512 devices in a mesh: row: 64 (over x, y_hi, z), col: 8 (over y_lo, core).
Axes of the slice: x: 4, y: 8 (y_hi: 2, y_lo: 4; y = y_hi * 4 + y_lo), z: 8, core: 2. Of those that a mesh axis runs over, the one named last changes fastest.
Arguments:
- features: bfloat16 [8, 512, 256, 128], P(None, 'row', 'col'), may hold values from -6 to 6
- kernel_one: bfloat16 [3, 3, 3, 128, 128], replicated, may hold values from -0.109375 to 0.109375
- projection: bfloat16 [512, 256], replicated, may hold values from -0.25 to 0.25
- kernel_two: bfloat16 [3, 3, 3, 256, 256], replicated, may hold values from -0.078125 to 0.078125
Outputs:
- latent: bfloat16 [8, 256, 128, 256], P(None, 'row', 'col')
The draws below stay inside these ranges and needn't reach their ends.
All inputs are finite; a program needn't handle non-finite values.
Results may differ from the reference program's by a relative error of at most 0.017.
Values may be sent and summed in bfloat16 or wider, within the bound.
No kernel may reach another device: no remote copies, remote signals or barrier semaphores. Data moves between devices by JAX's collectives and lax.ppermute only.
A program may use at most 128 MiB of HBM per device.

```python
import jax
import jax.numpy as jnp
from jax import lax

WIDTH_ONE = 128
WIDTH_TWO = 256
FRAMES = 8
ROWS = 512
COLS = 256


def steps_of(rng, extent, shards, smallest, largest):
    def one(axis_at, parts):
        draws = jax.random.uniform(jax.random.fold_in(jax.random.fold_in(rng, 6), axis_at), (parts,), jnp.float32, smallest / len(shards), largest / len(shards))
        return jnp.repeat(jnp.exp(draws), extent[axis_at] // parts).reshape((-1,) + (1,) * (len(extent) - axis_at - 1))

    factor_of = one(*shards[0])
    for cut in shards[1:]:
        factor_of = factor_of * one(*cut)
    return factor_of


def centred(key, dims, spread, most, split=(), dtype=jnp.bfloat16):
    entries = spread * jax.random.normal(key, dims, jnp.float32)
    if split:
        entries = entries * steps_of(key, dims, split, -0.22, 0.18)
    return jnp.clip(entries, -most, most).astype(dtype)


def setup_inputs(seed: int = 0) -> dict:
    seeds = jax.random.split(jax.random.key(seed), 5)
    return {
        "features": centred(seeds[0], (FRAMES, ROWS, COLS, WIDTH_ONE), 1.0, 6.0, ((1, 64), (2, 8))),
        "kernel_one": centred(seeds[1], (3, 3, 3, WIDTH_ONE, WIDTH_ONE), (27 * WIDTH_ONE) ** -0.5, 0.109375),
        "projection": centred(seeds[2], (4 * WIDTH_ONE, WIDTH_TWO), (4 * WIDTH_ONE) ** -0.5, 0.25),
        "kernel_two": centred(seeds[3], (3, 3, 3, WIDTH_TWO, WIDTH_TWO), (27 * WIDTH_TWO) ** -0.5, 0.078125),
    }


NORM_EPS = 1e-06

def normed_silu(values):
    widened = values.astype(jnp.float32)
    scaled = widened * lax.rsqrt(lax.optimization_barrier(jnp.mean(widened * widened, axis=-1, keepdims=True)) + NORM_EPS)
    return jax.nn.silu(scaled).astype(jnp.bfloat16)

def causal_conv(active, kernel):
    frame_count, row_count, col_count, channels = active.shape
    padded = jnp.pad(active, ((2, 0), (1, 1), (1, 1), (0, 0))).astype(jnp.float32)
    weights = kernel.astype(jnp.float32)
    summed = jnp.zeros((frame_count * row_count * col_count, kernel.shape[-1]), jnp.float32)
    for tap_t in range(3):
        for tap_r in range(3):
            for tap_c in range(3):
                window = padded[tap_t:tap_t + frame_count, tap_r:tap_r + row_count, tap_c:tap_c + col_count]
                summed = summed + jnp.dot(window.reshape(-1, channels), weights[tap_t, tap_r, tap_c])
    return summed.reshape(frame_count, row_count, col_count, -1)

def haar_bands(values):
    widened = values.astype(jnp.float32)
    upper = widened[:, 0::2]
    lower = widened[:, 1::2]
    first = upper[:, :, 0::2]
    second = upper[:, :, 1::2]
    third = lower[:, :, 0::2]
    fourth = lower[:, :, 1::2]
    low_pass = (first + second + third + fourth) * 0.5
    across = (first + second - third - fourth) * 0.5
    along = (first - second + third - fourth) * 0.5
    diagonal = (first - second - third + fourth) * 0.5
    return jnp.concatenate([low_pass, across, along, diagonal], axis=-1).astype(jnp.bfloat16)

def level_two_input(bands, projection):
    width_one = bands.shape[-1] // 4
    low_pass = bands[..., :width_one].astype(jnp.float32)
    flat = bands.reshape(-1, bands.shape[-1])
    mixed = jnp.dot(flat, projection, preferred_element_type=jnp.float32)
    mixed = mixed.reshape(bands.shape[:3] + (projection.shape[-1],))
    return (mixed + jnp.concatenate([low_pass, low_pass], axis=-1)).astype(jnp.bfloat16)

def reference(features, kernel_one, projection, kernel_two):
    active_one = normed_silu(features)
    level_one = (features.astype(jnp.float32) + causal_conv(active_one, kernel_one)).astype(jnp.bfloat16)
    bands = haar_bands(level_one)
    level_two = level_two_input(bands, projection)
    active_two = normed_silu(level_two)
    return (level_two.astype(jnp.float32) + causal_conv(active_two, kernel_two)).astype(jnp.bfloat16)
```

```python
import jax
import jax.numpy as jnp
from jax import lax
from jax.experimental import pallas as pl
from jax.experimental.pallas import tpu as pltpu
from jax.sharding import PartitionSpec as P

NORM_EPS = 1e-06
FR, RW, CL, C1, C2 = 8, 8, 32, 128, 256
HALO = 3
BF, F32 = jnp.bfloat16, jnp.float32
PITCH = 48
COLS_OF = (1, 2, 0, 3)
VM = pl.BlockSpec(memory_space=pltpu.VMEM)


def dot(a, b):
    return jnp.dot(a, b, preferred_element_type=F32)


def normed_silu(x, ones):
    mean = dot((x * x).astype(BF), ones)
    half = x * (0.5 * lax.rsqrt(mean + NORM_EPS))
    return half + half * jnp.tanh(half)


def mean_matrix(n):
    return jnp.full((n, n), 1.0 / n, BF)


def build_weights(k1, proj, w, m):
    p0, p1, p2, p3 = (proj[i * C1 : (i + 1) * C1].astype(F32) * 0.5 for i in range(4))
    row = lax.broadcasted_iota(jnp.int32, (C1, C2), 0)
    col = lax.broadcasted_iota(jnp.int32, (C1, C2), 1)
    twice = jnp.where((col == row) | (col == row + C1), 0.5, 0.0).astype(F32)
    m[0:C1] = (p0 + p1 + p2 + p3 + twice).astype(BF)
    m[C1 : 2 * C1] = (p0 + p1 - p2 - p3 + twice).astype(BF)
    m[2 * C1 : 3 * C1] = (p0 - p1 + p2 - p3 + twice).astype(BF)
    m[3 * C1 : 4 * C1] = (p0 - p1 - p2 + p3 + twice).astype(BF)
    zero = jnp.zeros((C1, C1), BF)

    def tap(p, q, s):
        return k1[p, q, s] if 0 <= s < 3 else zero

    for p in range(3):
        for dr in range(4):
            pairs = [pr for pr in range(2) if 0 <= dr - pr < 3]
            left = jnp.concatenate(
                [
                    jnp.concatenate([tap(p, dr - pr, dc - pc) for pr in pairs for pc in range(2)], axis=1)
                    for dc in COLS_OF
                ],
                axis=0,
            )
            w[p, dr] = dot(left, m[pairs[0] * 256 : (pairs[-1] + 1) * 256]).astype(BF)


def lay_out(feature, row_of, ones, wide, plain, a, b, c, f):
    rows = len(row_of)
    span = rows * PITCH
    for t in range(2):
        for r, at in enumerate(row_of):
            base = t * span + r * PITCH
            wide[base + 8 : base + 16] = jnp.zeros((8, C1), F32)
            wide[base + 32 : base + 40] = jnp.zeros((8, C1), F32)
            a[t, at] = jnp.zeros((16, C2), BF)
            b[t, at] = jnp.zeros((16, C2), BF)
    for t in range(FR):
        x = feature(t).astype(F32)
        act = normed_silu(x, ones)
        for r, at in enumerate(row_of):
            base = (t + 2) * span + r * PITCH
            wide[base : base + 8] = jnp.zeros((8, C1), F32)
            wide[base + 40 : base + 48] = jnp.zeros((8, C1), F32)
            wide[base + 8 : base + 40] = act[r * CL : (r + 1) * CL]
            own = (t * rows + r) * CL
            plain[own : own + CL] = x[r * CL : (r + 1) * CL]
            a[t + 2, at, :, 0:C1] = wide[pl.ds(base + 8, 16, stride=2), :].astype(BF)
            a[t + 2, at, :, C1:C2] = wide[pl.ds(base + 9, 16, stride=2), :].astype(BF)
            b[t + 2, at, :, 0:C1] = wide[pl.ds(base + 7, 16, stride=2), :].astype(BF)
            b[t + 2, at, :, C1:C2] = wide[pl.ds(base + 10, 16, stride=2), :].astype(BF)
            f[t, at, :, 0:C1] = plain[pl.ds(own, 16, stride=2), :].astype(BF)
            f[t, at, :, C1:C2] = plain[pl.ds(own + 1, 16, stride=2), :].astype(BF)
    zero = jnp.zeros((FR, C1), F32)
    for p in range(3):
        for r, at in enumerate(row_of):
            base = p * span + r * PITCH + 8
            first = wide[pl.ds(base, FR, stride=span), :]
            last = wide[pl.ds(base + CL - 1, FR, stride=span), :]
            c[p, at, :, 0:C1] = jnp.concatenate([zero, last], axis=0).astype(BF)
            c[p, at, :, C1:C2] = jnp.concatenate([first, zero], axis=0).astype(BF)


def contribute(i, have, slot, w, m, a, b, f):
    total = None
    taps = [dr for dr in range(4) if 2 * i + dr in have]
    for p in range(3):
        left = jnp.concatenate(
            [src[p : p + FR, slot(2 * i + dr)].reshape(FR * 16, C2) for dr in taps for src in (a, b)], axis=1
        )
        right = w[p, taps[0] : taps[-1] + 1].reshape(len(taps) * 512, C2)
        got = dot(left, right)
        total = got if total is None else total + got
    for pr in range(2):
        if 2 * i + 1 + pr in have:
            total = total + dot(f[:, slot(2 * i + 1 + pr)].reshape(FR * 16, C2), m[pr * 256 : (pr + 1) * 256])
    return total


def ring(i_rows, have, slot, w, c):
    total = None
    blank = jnp.zeros((16, C2), BF)
    for dr in range(4):
        if not any(2 * i + dr in have for i in i_rows):
            continue
        for p in range(3):
            left = jnp.concatenate([c[p, slot(2 * i + dr)] if 2 * i + dr in have else blank for i in i_rows], axis=0)
            got = dot(left, w[p, dr, 256:512])
            total = got if total is None else total + got
    return total


def put(acc, i, got, old=None):
    for h in range(2):
        new = got[:, h * 128 : (h + 1) * 128].reshape(FR, 16, 128)
        acc[h, :, i] = new if old is None else old[h, :, i] + new


def own_kernel(feat, k1, proj, w, m, acc, edge, wide, plain, a, b, c, f):
    build_weights(k1, proj, w, m)
    ones = mean_matrix(C1)
    lay_out(lambda t: feat[t].reshape(RW * CL, C1), range(RW), ones, wide, plain, a, b, c, f)
    have = range(HALO, HALO + RW)

    def slot(r):
        return r - HALO

    for i in range(6):
        put(acc, i, contribute(i, have, slot, w, m, a, b, f))
    edge[...] = ring(range(6), have, slot, w, c)


HALO_ROWS = (0, 1, 2, 11, 12, 13)


def halo_kernel(place, from_b, from_a, w, m, acc_in, edge_in, acc, edge, to_b, to_a, joined, wide, plain, a, b, c, f):
    odd = place[0] % 2 == 1
    for t in range(FR):
        fb, fa = from_b[t], from_a[t]
        joined[t, 0:HALO] = jnp.where(odd, fa, fb)
        joined[t, HALO : 2 * HALO] = jnp.where(odd, fb, fa)
    ones = mean_matrix(C1)
    lay_out(lambda t: joined[t].reshape(2 * HALO * CL, C1), range(2 * HALO), ones, wide, plain, a, b, c, f)
    slot = HALO_ROWS.index
    for i in range(6):
        if any(2 * i + dr in HALO_ROWS for dr in range(4)):
            put(acc, i, contribute(i, HALO_ROWS, slot, w, m, a, b, f), acc_in)
        else:
            acc[:, :, i] = acc_in[:, :, i]
    edge[...] = edge_in[...] + ring(range(6), HALO_ROWS, slot, w, c)
    odd = place[1] % 2 == 1
    flat = acc.reshape(2 * FR * 6 * 16, 128)

    def column(i, j):
        return jnp.concatenate(
            [flat[pl.ds(h * 768 + i * 16 + j, FR, stride=96), :] for h in range(2)], axis=1
        )

    for i in range(6):
        right = jnp.concatenate([column(i, 15), edge[i * 16 + 8 : i * 16 + 16]], axis=0)
        left = jnp.concatenate([edge[i * 16 : i * 16 + 8], column(i, 0)], axis=0)
        to_b[i] = jnp.where(odd, right, left).astype(BF)
        to_a[i] = jnp.where(odd, left, right).astype(BF)


def final_kernel(last_row, last_col, place, from_b, pair, acc, edge_in, k2, out, lv, edge, wide, a2):
    odd = place[1] % 2 == 1
    for t in range(FR):
        for h in range(2):
            lv[h, t * 96 : (t + 1) * 96] = acc[h, t].reshape(96, 128)
    for i in range(6):
        fb = from_b[i].astype(F32)
        left = jnp.where(odd, pair[0, i].astype(F32), fb)
        right = jnp.where(odd, fb, pair[1, i].astype(F32))
        edge[i * 16 : i * 16 + 8] = edge_in[i * 16 : i * 16 + 8] + left[0:8]
        edge[i * 16 + 8 : i * 16 + 16] = edge_in[i * 16 + 8 : i * 16 + 16] + right[8:16]
        for h in range(2):
            half = slice(h * 128, (h + 1) * 128)
            lv[h, pl.ds(i * 16, FR, stride=96), :] += left[8:16, half]
            lv[h, pl.ds(i * 16 + 15, FR, stride=96), :] += right[0:8, half]
    def level(at, count):
        return jnp.concatenate([lv[0, at : at + count], lv[1, at : at + count]], axis=1)

    ones = mean_matrix(C2)
    keep = [jnp.float32(1.0)] * 6
    keep[0] = jnp.where(place[0] == 0, 0.0, 1.0)
    keep[5] = jnp.where(place[0] == last_row, 0.0, 1.0)
    keep_left = jnp.where(place[1] == 0, 0.0, 1.0)
    keep_right = jnp.where(place[1] == last_col, 0.0, 1.0)
    for t in range(FR):
        act = normed_silu(level(t * 96, 96), ones)
        for i in range(6):
            base = (t * 6 + i) * 32 + 8
            kept = act[i * 16 : (i + 1) * 16] * keep[i]
            for h in range(2):
                wide[h, base : base + 16] = kept[:, h * 128 : (h + 1) * 128]
    act = normed_silu(edge[...], ones)
    for i in range(6):
        for h in range(2):
            half = slice(h * 128, (h + 1) * 128)
            wide[h, pl.ds(i * 32 + 7, FR, stride=192), :] = act[i * 16 : i * 16 + 8, half] * (keep[i] * keep_left)
            wide[h, pl.ds(i * 32 + 24, FR, stride=192), :] = act[i * 16 + 8 : i * 16 + 16, half] * (
                keep[i] * keep_right
            )
    for s in range(3):
        for i in range(6):
            for t in range(2):
                a2[s, t, i] = jnp.zeros((16, C2), BF)
            for t in range(FR):
                base = (t * 6 + i) * 32 + 7 + s
                for h in range(2):
                    a2[s, t + 2, i, :, h * 128 : (h + 1) * 128] = wide[h, base : base + 16].astype(BF)
    for i in range(4):
        total = None
        for p in range(3):
            left = jnp.concatenate(
                [a2[s, p : p + FR, i + q].reshape(FR * 16, C2) for q in range(3) for s in range(3)], axis=1
            )
            got = dot(left, k2[p].reshape(9 * C2, C2))
            total = got if total is None else total + got
        for t in range(FR):
            at = (t * 6 + i + 1) * 16
            out[t, i] = (level(at, 16) + total[t * 16 : (t + 1) * 16]).astype(BF)


def in_vmem(shape, dtype):
    return jax.ShapeDtypeStruct(shape, dtype)


def operands(rows):
    return [
        pltpu.VMEM(((FR + 2) * rows * PITCH, C1), F32),
        pltpu.VMEM((FR * rows * CL, C1), F32),
        pltpu.VMEM((FR + 2, rows, 16, C2), BF),
        pltpu.VMEM((FR + 2, rows, 16, C2), BF),
        pltpu.VMEM((3, rows, 16, C2), BF),
        pltpu.VMEM((FR, rows, 16, C2), BF),
    ]


W_SHAPE = in_vmem((3, 4, 512, C2), BF)
M_SHAPE = in_vmem((512, C2), BF)
ACC_SHAPE = in_vmem((2, FR, 6, 16, 128), F32)
EDGE_SHAPE = in_vmem((96, C2), F32)
STRIP_SHAPE = in_vmem((6, 16, C2), BF)
SMEM = pl.BlockSpec(memory_space=pltpu.SMEM)
PARAMS = pltpu.CompilerParams(vmem_limit_bytes=40 * 2**20)


def own_part(feat, k1, proj):
    return pl.pallas_call(
        own_kernel,
        out_shape=(W_SHAPE, M_SHAPE, ACC_SHAPE, EDGE_SHAPE),
        in_specs=[VM] * 3,
        out_specs=(VM,) * 4,
        scratch_shapes=operands(RW),
        compiler_params=PARAMS,
        name="own_part",
    )(feat, k1, proj)


def halo_part(place, from_b, from_a, w, m, acc, edge):
    return pl.pallas_call(
        halo_kernel,
        out_shape=(ACC_SHAPE, EDGE_SHAPE, STRIP_SHAPE, STRIP_SHAPE),
        in_specs=[SMEM] + [VM] * 6,
        out_specs=(VM,) * 4,
        scratch_shapes=[pltpu.VMEM((FR, 2 * HALO, CL, C1), BF)] + operands(2 * HALO),
        compiler_params=PARAMS,
        name="halo_part",
    )(place, from_b, from_a, w, m, acc, edge)


def final_part(last_row, last_col, place, from_b, pair, acc, edge, k2):
    def kernel(*refs):
        final_kernel(last_row, last_col, *refs)

    return pl.pallas_call(
        kernel,
        out_shape=in_vmem((FR, 4, 16, C2), BF),
        in_specs=[SMEM] + [VM] * 5,
        out_specs=VM,
        scratch_shapes=[
            pltpu.VMEM((2, FR * 6 * 16, 128), F32),
            pltpu.VMEM((96, C2), F32),
            pltpu.VMEM((2, FR * 6 * 32, 128), F32),
            pltpu.VMEM((3, FR + 2, 6, 16, C2), BF),
        ],
        compiler_params=PARAMS,
        name="final_part",
    )(place, from_b, pair, acc, edge, k2)


def pairs(first, count):
    swaps = []
    for i in range(first, count - 1, 2):
        swaps += [(i, i + 1), (i + 1, i)]
    return swaps


def local(features, kernel_one, projection, kernel_two):
    rows, cols = lax.axis_size("row"), lax.axis_size("col")
    row, col = lax.axis_index("row"), lax.axis_index("col")
    place = jnp.stack([row, col]).astype(jnp.int32)
    last = RW - HALO
    odd = row % 2
    send_b = lax.dynamic_slice_in_dim(features, odd * last, HALO, axis=1)
    send_a = lax.dynamic_slice_in_dim(features, (1 - odd) * last, HALO, axis=1)
    from_b = lax.ppermute(send_b, "row", pairs(1, rows))
    from_a = lax.ppermute(send_a, "row", pairs(0, rows))
    w, m, acc, edge = own_part(features, kernel_one, projection)
    acc, edge, to_b, to_a = halo_part(place, from_b, from_a, w, m, acc, edge)
    from_b = lax.ppermute(to_b, "col", pairs(1, cols))
    pair = lax.all_gather(to_a, "col", axis_index_groups=[[i, i + 1] for i in range(0, cols, 2)])
    return final_part(rows - 1, cols - 1, place, from_b, pair, acc, edge, kernel_two)


def solution(mesh):
    return jax.shard_map(
        local,
        mesh=mesh,
        in_specs=(P(None, "row", "col", None), P(), P(), P()),
        out_specs=P(None, "row", "col", None),
        check_vma=False,
    )
```

```python
import jax
import jax.numpy as jnp
from jax import lax
from jax.experimental import pallas as pl
from jax.experimental.pallas import tpu as pltpu
from jax.sharding import PartitionSpec as P

NORM_EPS = 1e-06
FR, RW, CL, C1, C2 = 8, 8, 32, 128, 256
HALO = 3
BF, F32 = jnp.bfloat16, jnp.float32
PITCH = 48
COLS_OF = (1, 2, 0, 3)
VM = pl.BlockSpec(memory_space=pltpu.VMEM)


def dot(a, b):
    return jnp.dot(a, b, preferred_element_type=F32)


def normed_silu(x, ones):
    mean = dot((x * x).astype(BF), ones)
    half = x * (0.5 * lax.rsqrt(mean + NORM_EPS))
    return half + half * jnp.tanh(half)


def mean_matrix(n):
    return jnp.full((n, n), 1.0 / n, BF)


def build_weights(k1, proj, w, m):
    p0, p1, p2, p3 = (proj[i * C1 : (i + 1) * C1].astype(F32) * 0.5 for i in range(4))
    row = lax.broadcasted_iota(jnp.int32, (C1, C2), 0)
    col = lax.broadcasted_iota(jnp.int32, (C1, C2), 1)
    twice = jnp.where((col == row) | (col == row + C1), 0.5, 0.0).astype(F32)
    m[0:C1] = (p0 + p1 + p2 + p3 + twice).astype(BF)
    m[C1 : 2 * C1] = (p0 + p1 - p2 - p3 + twice).astype(BF)
    m[2 * C1 : 3 * C1] = (p0 - p1 + p2 - p3 + twice).astype(BF)
    m[3 * C1 : 4 * C1] = (p0 - p1 - p2 + p3 + twice).astype(BF)
    zero = jnp.zeros((C1, C1), BF)

    def tap(p, q, s):
        return k1[p, q, s] if 0 <= s < 3 else zero

    for p in range(3):
        for dr in range(4):
            pairs = [pr for pr in range(2) if 0 <= dr - pr < 3]
            left = jnp.concatenate(
                [
                    jnp.concatenate([tap(p, dr - pr, dc - pc) for pr in pairs for pc in range(2)], axis=1)
                    for dc in COLS_OF
                ],
                axis=0,
            )
            w[p, dr] = dot(left, m[pairs[0] * 256 : (pairs[-1] + 1) * 256]).astype(BF)


def lay_out(feature, row_of, ones, wide, plain, a, b, c, f):
    rows = len(row_of)
    span = rows * PITCH
    for t in range(2):
        for r, at in enumerate(row_of):
            base = t * span + r * PITCH
            wide[base + 8 : base + 16] = jnp.zeros((8, C1), F32)
            wide[base + 32 : base + 40] = jnp.zeros((8, C1), F32)
            a[t, at] = jnp.zeros((16, C2), BF)
            b[t, at] = jnp.zeros((16, C2), BF)
    for t in range(FR):
        x = feature(t).astype(F32)
        act = normed_silu(x, ones)
        for r, at in enumerate(row_of):
            base = (t + 2) * span + r * PITCH
            wide[base : base + 8] = jnp.zeros((8, C1), F32)
            wide[base + 40 : base + 48] = jnp.zeros((8, C1), F32)
            wide[base + 8 : base + 40] = act[r * CL : (r + 1) * CL]
            own = (t * rows + r) * CL
            plain[own : own + CL] = x[r * CL : (r + 1) * CL]
            a[t + 2, at, :, 0:C1] = wide[pl.ds(base + 8, 16, stride=2), :].astype(BF)
            a[t + 2, at, :, C1:C2] = wide[pl.ds(base + 9, 16, stride=2), :].astype(BF)
            b[t + 2, at, :, 0:C1] = wide[pl.ds(base + 7, 16, stride=2), :].astype(BF)
            b[t + 2, at, :, C1:C2] = wide[pl.ds(base + 10, 16, stride=2), :].astype(BF)
            f[t, at, :, 0:C1] = plain[pl.ds(own, 16, stride=2), :].astype(BF)
            f[t, at, :, C1:C2] = plain[pl.ds(own + 1, 16, stride=2), :].astype(BF)
    zero = jnp.zeros((FR, C1), F32)
    for p in range(3):
        for r, at in enumerate(row_of):
            base = p * span + r * PITCH + 8
            first = wide[pl.ds(base, FR, stride=span), :]
            last = wide[pl.ds(base + CL - 1, FR, stride=span), :]
            c[p, at, :, 0:C1] = jnp.concatenate([zero, last], axis=0).astype(BF)
            c[p, at, :, C1:C2] = jnp.concatenate([first, zero], axis=0).astype(BF)


def contribute(i, have, slot, w, m, a, b, f):
    total = None
    taps = [dr for dr in range(4) if 2 * i + dr in have]
    for p in range(3):
        left = jnp.concatenate(
            [src[p : p + FR, slot(2 * i + dr)].reshape(FR * 16, C2) for dr in taps for src in (a, b)], axis=1
        )
        right = w[p, taps[0] : taps[-1] + 1].reshape(len(taps) * 512, C2)
        got = dot(left, right)
        total = got if total is None else total + got
    for pr in range(2):
        if 2 * i + 1 + pr in have:
            total = total + dot(f[:, slot(2 * i + 1 + pr)].reshape(FR * 16, C2), m[pr * 256 : (pr + 1) * 256])
    return total


def ring(i_rows, have, slot, w, c):
    total = None
    blank = jnp.zeros((16, C2), BF)
    for dr in range(4):
        if not any(2 * i + dr in have for i in i_rows):
            continue
        for p in range(3):
            left = jnp.concatenate([c[p, slot(2 * i + dr)] if 2 * i + dr in have else blank for i in i_rows], axis=0)
            got = dot(left, w[p, dr, 256:512])
            total = got if total is None else total + got
    return total


def put(acc, i, got, old=None):
    for h in range(2):
        new = got[:, h * 128 : (h + 1) * 128].reshape(FR, 16, 128)
        acc[h, :, i] = new if old is None else old[h, :, i] + new


def own_kernel(feat, k1, proj, w, m, acc, edge, wide, plain, a, b, c, f):
    build_weights(k1, proj, w, m)
    ones = mean_matrix(C1)
    lay_out(lambda t: feat[t].reshape(RW * CL, C1), range(RW), ones, wide, plain, a, b, c, f)
    have = range(HALO, HALO + RW)

    def slot(r):
        return r - HALO

    for i in range(6):
        put(acc, i, contribute(i, have, slot, w, m, a, b, f))
    edge[...] = ring(range(6), have, slot, w, c)


HALO_ROWS = (0, 1, 2, 11, 12, 13)


def halo_kernel(place, from_b, from_a, w, m, acc_in, edge_in, acc, edge, to_b, to_a, joined, wide, plain, a, b, c, f):
    odd = place[0] % 2 == 1
    for t in range(FR):
        fb, fa = from_b[t], from_a[t]
        joined[t, 0:HALO] = jnp.where(odd, fa, fb)
        joined[t, HALO : 2 * HALO] = jnp.where(odd, fb, fa)
    ones = mean_matrix(C1)
    lay_out(lambda t: joined[t].reshape(2 * HALO * CL, C1), range(2 * HALO), ones, wide, plain, a, b, c, f)
    slot = HALO_ROWS.index
    for i in range(6):
        if any(2 * i + dr in HALO_ROWS for dr in range(4)):
            put(acc, i, contribute(i, HALO_ROWS, slot, w, m, a, b, f), acc_in)
        else:
            acc[:, :, i] = acc_in[:, :, i]
    edge[...] = edge_in[...] + ring(range(6), HALO_ROWS, slot, w, c)
    odd = place[1] % 2 == 1
    flat = acc.reshape(2 * FR * 6 * 16, 128)

    def column(i, j):
        return jnp.concatenate(
            [flat[pl.ds(h * 768 + i * 16 + j, FR, stride=96), :] for h in range(2)], axis=1
        )

    for i in range(6):
        right = jnp.concatenate([column(i, 15), edge[i * 16 + 8 : i * 16 + 16]], axis=0)
        left = jnp.concatenate([edge[i * 16 : i * 16 + 8], column(i, 0)], axis=0)
        to_b[i] = jnp.where(odd, right, left).astype(BF)
        to_a[i] = jnp.where(odd, left, right).astype(BF)


def final_kernel(last_row, last_col, place, from_b, pair, acc, edge_in, k2, out, lv, edge, wide, a2):
    odd = place[1] % 2 == 1
    for t in range(FR):
        for h in range(2):
            lv[h, t * 96 : (t + 1) * 96] = acc[h, t].reshape(96, 128)
    for i in range(6):
        fb = from_b[i].astype(F32)
        left = jnp.where(odd, pair[0, i].astype(F32), fb)
        right = jnp.where(odd, fb, pair[1, i].astype(F32))
        edge[i * 16 : i * 16 + 8] = edge_in[i * 16 : i * 16 + 8] + left[0:8]
        edge[i * 16 + 8 : i * 16 + 16] = edge_in[i * 16 + 8 : i * 16 + 16] + right[8:16]
        for h in range(2):
            half = slice(h * 128, (h + 1) * 128)
            lv[h, pl.ds(i * 16, FR, stride=96), :] += left[8:16, half]
            lv[h, pl.ds(i * 16 + 15, FR, stride=96), :] += right[0:8, half]
    def level(at, count):
        return jnp.concatenate([lv[0, at : at + count], lv[1, at : at + count]], axis=1)

    ones = mean_matrix(C2)
    keep = [jnp.float32(1.0)] * 6
    keep[0] = jnp.where(place[0] == 0, 0.0, 1.0)
    keep[5] = jnp.where(place[0] == last_row, 0.0, 1.0)
    keep_left = jnp.where(place[1] == 0, 0.0, 1.0)
    keep_right = jnp.where(place[1] == last_col, 0.0, 1.0)
    for t in range(FR):
        act = normed_silu(level(t * 96, 96), ones)
        for i in range(6):
            base = (t * 6 + i) * 32 + 8
            kept = act[i * 16 : (i + 1) * 16] * keep[i]
            for h in range(2):
                wide[h, base : base + 16] = kept[:, h * 128 : (h + 1) * 128]
    act = normed_silu(edge[...], ones)
    for i in range(6):
        for h in range(2):
            half = slice(h * 128, (h + 1) * 128)
            wide[h, pl.ds(i * 32 + 7, FR, stride=192), :] = act[i * 16 : i * 16 + 8, half] * (keep[i] * keep_left)
            wide[h, pl.ds(i * 32 + 24, FR, stride=192), :] = act[i * 16 + 8 : i * 16 + 16, half] * (
                keep[i] * keep_right
            )
    for s in range(3):
        for i in range(6):
            for t in range(2):
                a2[s, t, i] = jnp.zeros((16, C2), BF)
            for t in range(FR):
                base = (t * 6 + i) * 32 + 7 + s
                for h in range(2):
                    a2[s, t + 2, i, :, h * 128 : (h + 1) * 128] = wide[h, base : base + 16].astype(BF)
    for i in range(4):
        total = None
        for p in range(3):
            left = jnp.concatenate(
                [a2[s, p : p + FR, i + q].reshape(FR * 16, C2) for q in range(3) for s in range(3)], axis=1
            )
            got = dot(left, k2[p].reshape(9 * C2, C2))
            total = got if total is None else total + got
        for t in range(FR):
            at = (t * 6 + i + 1) * 16
            out[t, i] = (level(at, 16) + total[t * 16 : (t + 1) * 16]).astype(BF)


def in_vmem(shape, dtype):
    return jax.ShapeDtypeStruct(shape, dtype)


def operands(rows):
    return [
        pltpu.VMEM(((FR + 2) * rows * PITCH, C1), F32),
        pltpu.VMEM((FR * rows * CL, C1), F32),
        pltpu.VMEM((FR + 2, rows, 16, C2), BF),
        pltpu.VMEM((FR + 2, rows, 16, C2), BF),
        pltpu.VMEM((3, rows, 16, C2), BF),
        pltpu.VMEM((FR, rows, 16, C2), BF),
    ]


W_SHAPE = in_vmem((3, 4, 512, C2), BF)
M_SHAPE = in_vmem((512, C2), BF)
ACC_SHAPE = in_vmem((2, FR, 6, 16, 128), F32)
EDGE_SHAPE = in_vmem((96, C2), F32)
STRIP_SHAPE = in_vmem((6, 16, C2), BF)
SMEM = pl.BlockSpec(memory_space=pltpu.SMEM)
PARAMS = pltpu.CompilerParams(vmem_limit_bytes=40 * 2**20)


def stage_kernel(place, feat, k1, proj, send_b, send_a, feat_in, k1_in, proj_in, sems):
    odd = place[0] % 2
    last = RW - HALO
    moves = [
        (feat.at[:, pl.ds(odd * last, HALO)], send_b),
        (feat.at[:, pl.ds((1 - odd) * last, HALO)], send_a),
        (k1, k1_in),
        (proj, proj_in),
        (feat, feat_in),
    ]
    copies = [pltpu.make_async_copy(src, dst, sems.at[n]) for n, (src, dst) in enumerate(moves)]
    for copy in copies:
        copy.start()
    for copy in copies:
        copy.wait()


def stage(place, feat, k1, proj):
    strip = in_vmem((FR, HALO, CL, C1), BF)
    return pl.pallas_call(
        stage_kernel,
        out_shape=(strip, strip) + tuple(in_vmem(x.shape, x.dtype) for x in (feat, k1, proj)),
        in_specs=[SMEM] + [pl.BlockSpec(memory_space=pltpu.HBM)] * 3,
        out_specs=(VM,) * 5,
        scratch_shapes=[pltpu.SemaphoreType.DMA((5,))],
        compiler_params=PARAMS,
        name="stage",
    )(place, *(pltpu.with_memory_space_constraint(x, pltpu.HBM) for x in (feat, k1, proj)))


def own_part(feat, k1, proj):
    return pl.pallas_call(
        own_kernel,
        out_shape=(W_SHAPE, M_SHAPE, ACC_SHAPE, EDGE_SHAPE),
        in_specs=[VM] * 3,
        out_specs=(VM,) * 4,
        scratch_shapes=operands(RW),
        compiler_params=PARAMS,
        name="own_part",
    )(feat, k1, proj)


def halo_part(place, from_b, from_a, w, m, acc, edge):
    return pl.pallas_call(
        halo_kernel,
        out_shape=(ACC_SHAPE, EDGE_SHAPE, STRIP_SHAPE, STRIP_SHAPE),
        in_specs=[SMEM] + [VM] * 6,
        out_specs=(VM,) * 4,
        scratch_shapes=[pltpu.VMEM((FR, 2 * HALO, CL, C1), BF)] + operands(2 * HALO),
        compiler_params=PARAMS,
        name="halo_part",
    )(place, from_b, from_a, w, m, acc, edge)


def final_part(last_row, last_col, place, from_b, pair, acc, edge, k2):
    def kernel(*refs):
        final_kernel(last_row, last_col, *refs)

    return pl.pallas_call(
        kernel,
        out_shape=in_vmem((FR, 4, 16, C2), BF),
        in_specs=[SMEM] + [VM] * 5,
        out_specs=VM,
        scratch_shapes=[
            pltpu.VMEM((2, FR * 6 * 16, 128), F32),
            pltpu.VMEM((96, C2), F32),
            pltpu.VMEM((2, FR * 6 * 32, 128), F32),
            pltpu.VMEM((3, FR + 2, 6, 16, C2), BF),
        ],
        compiler_params=PARAMS,
        name="final_part",
    )(place, from_b, pair, acc, edge, k2)


def pairs(first, count):
    swaps = []
    for i in range(first, count - 1, 2):
        swaps += [(i, i + 1), (i + 1, i)]
    return swaps


def local(features, kernel_one, projection, kernel_two):
    rows, cols = lax.axis_size("row"), lax.axis_size("col")
    row, col = lax.axis_index("row"), lax.axis_index("col")
    place = jnp.stack([row, col]).astype(jnp.int32)
    send_b, send_a, features, kernel_one, projection = stage(place, features, kernel_one, projection)
    from_b = lax.ppermute(send_b, "row", pairs(1, rows))
    from_a = lax.ppermute(send_a, "row", pairs(0, rows))
    w, m, acc, edge = own_part(features, kernel_one, projection)
    acc, edge, to_b, to_a = halo_part(place, from_b, from_a, w, m, acc, edge)
    from_b = lax.ppermute(to_b, "col", pairs(1, cols))
    pair = lax.all_gather(to_a, "col", axis_index_groups=[[i, i + 1] for i in range(0, cols, 2)])
    return final_part(rows - 1, cols - 1, place, from_b, pair, acc, edge, kernel_two)


def solution(mesh):
    return jax.shard_map(
        local,
        mesh=mesh,
        in_specs=(P(None, "row", "col", None), P(), P(), P()),
        out_specs=P(None, "row", "col", None),
        check_vma=False,
    )
```

```python
import jax
import jax.numpy as jnp
from jax import lax
from jax.experimental import pallas as pl
from jax.experimental.pallas import tpu as pltpu
from jax.sharding import PartitionSpec as P

NORM_EPS = 1e-06
FR, RW, CL, C1, C2 = 8, 8, 32, 128, 256
HALO = 3
BF, F32 = jnp.bfloat16, jnp.float32
PITCH = 48
COLS_OF = (1, 2, 0, 3)
FAR = 8
VM = pl.BlockSpec(memory_space=pltpu.VMEM)
HBM = pl.BlockSpec(memory_space=pltpu.HBM)


def dot(a, b):
    return jnp.dot(a, b, preferred_element_type=F32)


def normed_silu(x, ones):
    mean = dot((x * x).astype(BF), ones)
    half = x * (0.5 * lax.rsqrt(mean + NORM_EPS))
    return half + half * jnp.tanh(half)


def mean_matrix(n):
    return jnp.full((n, n), 1.0 / n, BF)


def build_weights(k1, proj, w, m):
    p0, p1, p2, p3 = (proj[i * C1 : (i + 1) * C1].astype(F32) * 0.5 for i in range(4))
    row = lax.broadcasted_iota(jnp.int32, (C1, C2), 0)
    col = lax.broadcasted_iota(jnp.int32, (C1, C2), 1)
    twice = jnp.where((col == row) | (col == row + C1), 0.5, 0.0).astype(F32)
    m[0:C1] = (p0 + p1 + p2 + p3 + twice).astype(BF)
    m[C1 : 2 * C1] = (p0 + p1 - p2 - p3 + twice).astype(BF)
    m[2 * C1 : 3 * C1] = (p0 - p1 + p2 - p3 + twice).astype(BF)
    m[3 * C1 : 4 * C1] = (p0 - p1 - p2 + p3 + twice).astype(BF)
    zero = jnp.zeros((C1, C1), BF)

    def tap(p, q, s):
        return k1[p, q, s] if 0 <= s < 3 else zero

    for p in range(3):
        for dr in range(4):
            pairs = [pr for pr in range(2) if 0 <= dr - pr < 3]
            left = jnp.concatenate(
                [
                    jnp.concatenate([tap(p, dr - pr, dc - pc) for pr in pairs for pc in range(2)], axis=1)
                    for dc in COLS_OF
                ],
                axis=0,
            )
            w[p, dr] = dot(left, m[pairs[0] * 256 : (pairs[-1] + 1) * 256]).astype(BF)


def lay_out(feature, row_of, ones, wide, plain, a, b, c, f):
    rows = len(row_of)
    span = rows * PITCH
    for t in range(2):
        for r, at in enumerate(row_of):
            base = t * span + r * PITCH
            wide[base + 8 : base + 16] = jnp.zeros((8, C1), F32)
            wide[base + 32 : base + 40] = jnp.zeros((8, C1), F32)
            a[t, at] = jnp.zeros((16, C2), BF)
            b[t, at] = jnp.zeros((16, C2), BF)
    for t in range(FR):
        x = feature(t).astype(F32)
        act = normed_silu(x, ones)
        for r, at in enumerate(row_of):
            base = (t + 2) * span + r * PITCH
            wide[base : base + 8] = jnp.zeros((8, C1), F32)
            wide[base + 40 : base + 48] = jnp.zeros((8, C1), F32)
            wide[base + 8 : base + 40] = act[r * CL : (r + 1) * CL]
            own = (t * rows + r) * CL
            plain[own : own + CL] = x[r * CL : (r + 1) * CL]
            a[t + 2, at, :, 0:C1] = wide[pl.ds(base + 8, 16, stride=2), :].astype(BF)
            a[t + 2, at, :, C1:C2] = wide[pl.ds(base + 9, 16, stride=2), :].astype(BF)
            b[t + 2, at, :, 0:C1] = wide[pl.ds(base + 7, 16, stride=2), :].astype(BF)
            b[t + 2, at, :, C1:C2] = wide[pl.ds(base + 10, 16, stride=2), :].astype(BF)
            f[t, at, :, 0:C1] = plain[pl.ds(own, 16, stride=2), :].astype(BF)
            f[t, at, :, C1:C2] = plain[pl.ds(own + 1, 16, stride=2), :].astype(BF)
    zero = jnp.zeros((FR, C1), F32)
    for p in range(3):
        for r, at in enumerate(row_of):
            base = p * span + r * PITCH + 8
            first = wide[pl.ds(base, FR, stride=span), :]
            last = wide[pl.ds(base + CL - 1, FR, stride=span), :]
            c[p, at, :, 0:C1] = jnp.concatenate([zero, last], axis=0).astype(BF)
            c[p, at, :, C1:C2] = jnp.concatenate([first, zero], axis=0).astype(BF)


def contribute(i, have, slot, w, m, a, b, f):
    total = None
    taps = [dr for dr in range(4) if 2 * i + dr in have]
    for p in range(3):
        left = jnp.concatenate(
            [src[p : p + FR, slot(2 * i + dr)].reshape(FR * 16, C2) for dr in taps for src in (a, b)], axis=1
        )
        right = w[p, taps[0] : taps[-1] + 1].reshape(len(taps) * 512, C2)
        got = dot(left, right)
        total = got if total is None else total + got
    for pr in range(2):
        if 2 * i + 1 + pr in have:
            total = total + dot(f[:, slot(2 * i + 1 + pr)].reshape(FR * 16, C2), m[pr * 256 : (pr + 1) * 256])
    return total


def ring(i_rows, have, slot, w, c):
    total = None
    blank = jnp.zeros((16, C2), BF)
    for dr in range(4):
        if not any(2 * i + dr in have for i in i_rows):
            continue
        for p in range(3):
            left = jnp.concatenate([c[p, slot(2 * i + dr)] if 2 * i + dr in have else blank for i in i_rows], axis=0)
            got = dot(left, w[p, dr, 256:512])
            total = got if total is None else total + got
    return total


def put(acc, i, got, old=None):
    for h in range(2):
        new = got[:, h * 128 : (h + 1) * 128].reshape(FR, 16, 128)
        acc[h, :, i] = new if old is None else old[h, :, i] + new


def fetch(sources, targets, sems):
    copies = [pltpu.make_async_copy(a, b, sems.at[n]) for n, (a, b) in enumerate(zip(sources, targets, strict=True))]
    for copy in copies:
        copy.start()
    for copy in copies:
        copy.wait()


def early():
    return lax.axis_index("row") % FAR == 0


def first_kernel(feat, k1, proj, send_b, send_a, w, m, strip_sems, k1_in, proj_in, sems):
    last = (lax.axis_index("row") % 2) * (RW - HALO)
    copies = []
    for n, (begin, send) in enumerate([(last, send_b), (RW - HALO - last, send_a)]):
        copies += [
            pltpu.make_async_copy(feat.at[t, pl.ds(begin, HALO)], send.at[t], strip_sems.at[n, t]) for t in range(FR)
        ]
    for copy in copies:
        copy.start()
    for copy in copies:
        copy.wait()

    @pl.when(early())
    def _():
        fetch((k1, proj), (k1_in, proj_in), sems)
        build_weights(k1_in, proj_in, w, m)


def own_kernel(
    feat, k1, proj, w_in, m_in, w, m, acc, edge, k1_in, proj_in, feat_in, sems, feat_sem, wide, plain, a, b, c, f
):
    copy = pltpu.make_async_copy(feat, feat_in, feat_sem)
    copy.start()

    @pl.when(jnp.logical_not(early()))
    def _():
        fetch((k1, proj), (k1_in, proj_in), sems)
        build_weights(k1_in, proj_in, w, m)

    copy.wait()
    ones = mean_matrix(C1)
    lay_out(lambda t: feat_in[t].reshape(RW * CL, C1), range(RW), ones, wide, plain, a, b, c, f)
    have = range(HALO, HALO + RW)

    def slot(r):
        return r - HALO

    for i in range(6):
        put(acc, i, contribute(i, have, slot, w, m, a, b, f))
    edge[...] = ring(range(6), have, slot, w, c)


def add_side(low, got, w, m, acc_in, edge_in, acc, edge, wide, plain, a, b, c, f):
    lay_out(lambda t: got[t].reshape(HALO * CL, C1), range(HALO), mean_matrix(C1), wide, plain, a, b, c, f)
    whole, part = 5 * low, 1 + 3 * low
    one = 2 * (1 - low)

    def lines(src, p, r):
        return src[p : p + FR, r].reshape(FR * 16, C2)

    blank = jnp.zeros((16, C2), BF)
    total = beside = None
    for p in range(3):
        left = jnp.concatenate(
            [
                jnp.concatenate([lines(src, p, r), blank if src is a else c[p, r]], axis=0)
                for r in range(HALO)
                for src in (a, b)
            ],
            axis=1,
        )
        one_left = jnp.concatenate(
            [jnp.concatenate([lines(src, p, one), blank if src is a else c[p, one]], axis=0) for src in (a, b)], axis=1
        )
        here = dot(left, w[p, pl.ds(low, HALO)].reshape(HALO * 512, C2))
        there = dot(one_left, w[p, 3 * low])
        total = here if total is None else total + here
        beside = there if beside is None else beside + there
    skip = jnp.concatenate([f[:, 1 - low + n].reshape(FR * 16, C2) for n in range(2)], axis=1)
    main = total[0 : FR * 16] + dot(skip, m[...])
    for i, sums, rim in ((whole, main, total), (part, beside[0 : FR * 16], beside)):
        for h in range(2):
            acc[h, :, i] = acc_in[h, :, i] + sums[:, h * 128 : (h + 1) * 128].reshape(FR, 16, 128)
        at = pl.ds(pl.multiple_of(i * 16, 16), 16)
        edge[at] = edge_in[at] + rim[FR * 16 : FR * 16 + 16]


def beside_far():
    return lax.axis_index("row") % FAR < 2


def near_kernel(got, w, m, acc_in, edge_in, acc, edge, *scratch):
    @pl.when(beside_far())
    def _():
        add_side(1 - lax.axis_index("row") % 2, got, w, m, acc_in, edge_in, acc, edge, *scratch)


def far_kernel(got, got_near, w, m, acc_in, edge_in, acc, edge, to_b, to_a, *scratch):
    low = lax.axis_index("row") % 2

    @pl.when(jnp.logical_not(beside_far()))
    def _():
        add_side(1 - low, got_near, w, m, acc_in, edge_in, acc, edge, *scratch)

    add_side(low, got, w, m, acc_in, edge_in, acc, edge, *scratch)
    odd = lax.axis_index("col") % 2 == 1
    flat = acc.reshape(2 * FR * 6 * 16, 128)

    def column(i, j):
        return jnp.concatenate(
            [flat[pl.ds(h * 768 + i * 16 + j, FR, stride=96), :] for h in range(2)], axis=1
        )

    for i in range(6):
        right = jnp.concatenate([column(i, 15), edge[i * 16 + 8 : i * 16 + 16]], axis=0)
        left = jnp.concatenate([edge[i * 16 : i * 16 + 8], column(i, 0)], axis=0)
        to_b[i] = jnp.where(odd, right, left).astype(BF)
        to_a[i] = jnp.where(odd, left, right).astype(BF)


def final_kernel(last_row, last_col, from_b, pair, acc, edge_in, k2, out, lv, edge, wide, a2):
    row, col = lax.axis_index("row"), lax.axis_index("col")
    odd = col % 2 == 1
    for t in range(FR):
        for h in range(2):
            lv[h, t * 96 : (t + 1) * 96] = acc[h, t].reshape(96, 128)
    for i in range(6):
        fb = from_b[i].astype(F32)
        left = jnp.where(odd, pair[0, i].astype(F32), fb)
        right = jnp.where(odd, fb, pair[1, i].astype(F32))
        edge[i * 16 : i * 16 + 8] = edge_in[i * 16 : i * 16 + 8] + left[0:8]
        edge[i * 16 + 8 : i * 16 + 16] = edge_in[i * 16 + 8 : i * 16 + 16] + right[8:16]
        for h in range(2):
            half = slice(h * 128, (h + 1) * 128)
            lv[h, pl.ds(i * 16, FR, stride=96), :] += left[8:16, half]
            lv[h, pl.ds(i * 16 + 15, FR, stride=96), :] += right[0:8, half]
    def level(at, count):
        return jnp.concatenate([lv[0, at : at + count], lv[1, at : at + count]], axis=1)

    ones = mean_matrix(C2)
    keep = [jnp.float32(1.0)] * 6
    keep[0] = jnp.where(row == 0, 0.0, 1.0)
    keep[5] = jnp.where(row == last_row, 0.0, 1.0)
    keep_left = jnp.where(col == 0, 0.0, 1.0)
    keep_right = jnp.where(col == last_col, 0.0, 1.0)
    for t in range(FR):
        act = normed_silu(level(t * 96, 96), ones)
        for i in range(6):
            base = (t * 6 + i) * 32 + 8
            kept = act[i * 16 : (i + 1) * 16] * keep[i]
            for h in range(2):
                wide[h, base : base + 16] = kept[:, h * 128 : (h + 1) * 128]
    act = normed_silu(edge[...], ones)
    for i in range(6):
        for h in range(2):
            half = slice(h * 128, (h + 1) * 128)
            wide[h, pl.ds(i * 32 + 7, FR, stride=192), :] = act[i * 16 : i * 16 + 8, half] * (keep[i] * keep_left)
            wide[h, pl.ds(i * 32 + 24, FR, stride=192), :] = act[i * 16 + 8 : i * 16 + 16, half] * (
                keep[i] * keep_right
            )
    for s in range(3):
        for i in range(6):
            for t in range(2):
                a2[s, t, i] = jnp.zeros((16, C2), BF)
            for t in range(FR):
                base = (t * 6 + i) * 32 + 7 + s
                for h in range(2):
                    a2[s, t + 2, i, :, h * 128 : (h + 1) * 128] = wide[h, base : base + 16].astype(BF)
    for i in range(4):
        total = None
        for p in range(3):
            left = jnp.concatenate(
                [a2[s, p : p + FR, i + q].reshape(FR * 16, C2) for q in range(3) for s in range(3)], axis=1
            )
            got = dot(left, k2[p].reshape(9 * C2, C2))
            total = got if total is None else total + got
        for t in range(FR):
            at = (t * 6 + i + 1) * 16
            out[t, i] = (level(at, 16) + total[t * 16 : (t + 1) * 16]).astype(BF)


def in_vmem(shape, dtype):
    return jax.ShapeDtypeStruct(shape, dtype)


def operands(rows):
    return [
        pltpu.VMEM(((FR + 2) * rows * PITCH, C1), F32),
        pltpu.VMEM((FR * rows * CL, C1), F32),
        pltpu.VMEM((FR + 2, rows, 16, C2), BF),
        pltpu.VMEM((FR + 2, rows, 16, C2), BF),
        pltpu.VMEM((3, rows, 16, C2), BF),
        pltpu.VMEM((FR, rows, 16, C2), BF),
    ]


ROWS_SHAPE = in_vmem((FR, HALO, CL, C1), BF)
W_SHAPE = in_vmem((3, 4, 512, C2), BF)
M_SHAPE = in_vmem((512, C2), BF)
ACC_SHAPE = in_vmem((2, FR, 6, 16, 128), F32)
EDGE_SHAPE = in_vmem((96, C2), F32)
STRIP_SHAPE = in_vmem((6, 16, C2), BF)
PARAMS = pltpu.CompilerParams(vmem_limit_bytes=24 * 2**20)


def in_hbm(x):
    return pltpu.with_memory_space_constraint(x, pltpu.HBM)


def weight_scratch():
    return [
        pltpu.VMEM((3, 3, 3, C1, C1), BF),
        pltpu.VMEM((4 * C1, C2), BF),
    ]


def first_part(feat, k1, proj):
    return pl.pallas_call(
        first_kernel,
        out_shape=(ROWS_SHAPE,) * 2 + (W_SHAPE, M_SHAPE),
        in_specs=[HBM] * 3,
        out_specs=(VM,) * 4,
        scratch_shapes=[pltpu.SemaphoreType.DMA((2, FR))] + weight_scratch() + [pltpu.SemaphoreType.DMA((2,))],
        compiler_params=PARAMS,
        name="first_part",
    )(in_hbm(feat), in_hbm(k1), in_hbm(proj))


def own_part(feat, k1, proj, w, m):
    return pl.pallas_call(
        own_kernel,
        out_shape=(W_SHAPE, M_SHAPE, ACC_SHAPE, EDGE_SHAPE),
        in_specs=[HBM] * 3 + [VM] * 2,
        out_specs=(VM,) * 4,
        scratch_shapes=weight_scratch()
        + [pltpu.VMEM((FR, RW, CL, C1), BF), pltpu.SemaphoreType.DMA((2,)), pltpu.SemaphoreType.DMA]
        + operands(RW),
        input_output_aliases={3: 0, 4: 1},
        compiler_params=PARAMS,
        name="own_part",
    )(in_hbm(feat), in_hbm(k1), in_hbm(proj), w, m)


def near_part(got, w, m, acc, edge):
    return pl.pallas_call(
        near_kernel,
        out_shape=(ACC_SHAPE, EDGE_SHAPE),
        in_specs=[VM] * 5,
        out_specs=(VM,) * 2,
        scratch_shapes=operands(HALO),
        input_output_aliases={3: 0, 4: 1},
        compiler_params=PARAMS,
        name="near_part",
    )(got, w, m, acc, edge)


def far_part(got, got_near, w, m, acc, edge):
    return pl.pallas_call(
        far_kernel,
        out_shape=(ACC_SHAPE, EDGE_SHAPE, STRIP_SHAPE, STRIP_SHAPE),
        in_specs=[VM] * 6,
        out_specs=(VM,) * 4,
        scratch_shapes=operands(HALO),
        input_output_aliases={4: 0, 5: 1},
        compiler_params=PARAMS,
        name="far_part",
    )(got, got_near, w, m, acc, edge)


def final_part(last_row, last_col, from_b, pair, acc, edge, k2):
    def kernel(*refs):
        final_kernel(last_row, last_col, *refs)

    return pl.pallas_call(
        kernel,
        out_shape=in_vmem((FR, 4, 16, C2), BF),
        in_specs=[VM] * 5,
        out_specs=VM,
        scratch_shapes=[
            pltpu.VMEM((2, FR * 6 * 16, 128), F32),
            pltpu.VMEM((96, C2), F32),
            pltpu.VMEM((2, FR * 6 * 32, 128), F32),
            pltpu.VMEM((3, FR + 2, 6, 16, C2), BF),
        ],
        compiler_params=PARAMS,
        name="final_part",
    )(from_b, pair, acc, edge, k2)


def pairs(first, count):
    swaps = []
    for i in range(first, count - 1, 2):
        swaps += [(i, i + 1), (i + 1, i)]
    return swaps


def local(features, kernel_one, projection, kernel_two):
    rows, cols = lax.axis_size("row"), lax.axis_size("col")
    send_b, send_a, w, m = first_part(features, kernel_one, projection)
    far_side = [(i, j) for i, j in pairs(0, rows) if min(i, j) % FAR == 0]
    others = [pair for pair in pairs(0, rows) if pair not in far_side]
    from_a = lax.ppermute(send_a, "row", far_side)
    from_b = lax.ppermute(send_b, "row", pairs(1, rows))
    from_a_too = lax.ppermute(send_a, "row", others)
    w, m, acc, edge = own_part(features, kernel_one, projection, w, m)
    acc, edge = near_part(from_a, w, m, acc, edge)
    acc, edge, to_b, to_a = far_part(from_b, from_a_too, w, m, acc, edge)
    from_b = lax.ppermute(to_b, "col", pairs(1, cols))
    pair = lax.all_gather(to_a, "col", axis_index_groups=[[i, i + 1] for i in range(0, cols, 2)])
    return final_part(rows - 1, cols - 1, from_b, pair, acc, edge, kernel_two)


def solution(mesh):
    return jax.shard_map(
        local,
        mesh=mesh,
        in_specs=(P(None, "row", "col", None), P(), P(), P()),
        out_specs=P(None, "row", "col", None),
        check_vma=False,
    )
```

```python
import jax
import jax.numpy as jnp
from jax import lax
from jax.experimental import pallas as pl
from jax.experimental.pallas import tpu as pltpu
from jax.sharding import PartitionSpec as P

NORM_EPS = 1e-06
FR, RW, CL, C1, C2 = 8, 8, 32, 128, 256
HALO = 3
BF, F32 = jnp.bfloat16, jnp.float32
PITCH = 48
COLS_OF = (1, 2, 0, 3)
FAR = 8
VM = pl.BlockSpec(memory_space=pltpu.VMEM)
HBM = pl.BlockSpec(memory_space=pltpu.HBM)


def dot(a, b):
    return jnp.dot(a, b, preferred_element_type=F32)


def normed_silu(x, ones):
    mean = dot((x * x).astype(BF), ones)
    half = x * (0.5 * lax.rsqrt(mean + NORM_EPS))
    return half + half * jnp.tanh(half)


def mean_matrix(n):
    return jnp.full((n, n), 1.0 / n, BF)


def build_weights(k1, proj, w, m):
    p0, p1, p2, p3 = (proj[i * C1 : (i + 1) * C1].astype(F32) * 0.5 for i in range(4))
    row = lax.broadcasted_iota(jnp.int32, (C1, C2), 0)
    col = lax.broadcasted_iota(jnp.int32, (C1, C2), 1)
    twice = jnp.where((col == row) | (col == row + C1), 0.5, 0.0).astype(F32)
    m[0:C1] = (p0 + p1 + p2 + p3 + twice).astype(BF)
    m[C1 : 2 * C1] = (p0 + p1 - p2 - p3 + twice).astype(BF)
    m[2 * C1 : 3 * C1] = (p0 - p1 + p2 - p3 + twice).astype(BF)
    m[3 * C1 : 4 * C1] = (p0 - p1 - p2 + p3 + twice).astype(BF)
    zero = jnp.zeros((C1, C1), BF)

    def tap(p, q, s):
        return k1[p, q, s] if 0 <= s < 3 else zero

    for p in range(3):
        for dr in range(4):
            pairs = [pr for pr in range(2) if 0 <= dr - pr < 3]
            left = jnp.concatenate(
                [
                    jnp.concatenate([tap(p, dr - pr, dc - pc) for pr in pairs for pc in range(2)], axis=1)
                    for dc in COLS_OF
                ],
                axis=0,
            )
            w[p, dr] = dot(left, m[pairs[0] * 256 : (pairs[-1] + 1) * 256]).astype(BF)


def lay_out(feature, row_of, ones, wide, plain, a, b, c, f):
    rows = len(row_of)
    span = rows * PITCH
    for t in range(2):
        for r, at in enumerate(row_of):
            base = t * span + r * PITCH
            wide[base + 8 : base + 16] = jnp.zeros((8, C1), F32)
            wide[base + 32 : base + 40] = jnp.zeros((8, C1), F32)
            a[t, at] = jnp.zeros((16, C2), BF)
            b[t, at] = jnp.zeros((16, C2), BF)
    for t in range(FR):
        x = feature(t).astype(F32)
        act = normed_silu(x, ones)
        for r, at in enumerate(row_of):
            base = (t + 2) * span + r * PITCH
            wide[base : base + 8] = jnp.zeros((8, C1), F32)
            wide[base + 40 : base + 48] = jnp.zeros((8, C1), F32)
            wide[base + 8 : base + 40] = act[r * CL : (r + 1) * CL]
            own = (t * rows + r) * CL
            plain[own : own + CL] = x[r * CL : (r + 1) * CL]
            a[t + 2, at, :, 0:C1] = wide[pl.ds(base + 8, 16, stride=2), :].astype(BF)
            a[t + 2, at, :, C1:C2] = wide[pl.ds(base + 9, 16, stride=2), :].astype(BF)
            b[t + 2, at, :, 0:C1] = wide[pl.ds(base + 7, 16, stride=2), :].astype(BF)
            b[t + 2, at, :, C1:C2] = wide[pl.ds(base + 10, 16, stride=2), :].astype(BF)
            f[t, at, :, 0:C1] = plain[pl.ds(own, 16, stride=2), :].astype(BF)
            f[t, at, :, C1:C2] = plain[pl.ds(own + 1, 16, stride=2), :].astype(BF)
    zero = jnp.zeros((FR, C1), F32)
    for p in range(3):
        for r, at in enumerate(row_of):
            base = p * span + r * PITCH + 8
            first = wide[pl.ds(base, FR, stride=span), :]
            last = wide[pl.ds(base + CL - 1, FR, stride=span), :]
            c[p, at, :, 0:C1] = jnp.concatenate([zero, last], axis=0).astype(BF)
            c[p, at, :, C1:C2] = jnp.concatenate([first, zero], axis=0).astype(BF)


def contribute(i, have, slot, w, m, a, b, f):
    total = None
    taps = [dr for dr in range(4) if 2 * i + dr in have]
    for p in range(3):
        left = jnp.concatenate(
            [src[p : p + FR, slot(2 * i + dr)].reshape(FR * 16, C2) for dr in taps for src in (a, b)], axis=1
        )
        right = w[p, taps[0] : taps[-1] + 1].reshape(len(taps) * 512, C2)
        got = dot(left, right)
        total = got if total is None else total + got
    for pr in range(2):
        if 2 * i + 1 + pr in have:
            total = total + dot(f[:, slot(2 * i + 1 + pr)].reshape(FR * 16, C2), m[pr * 256 : (pr + 1) * 256])
    return total


def ring(i_rows, have, slot, w, c):
    total = None
    blank = jnp.zeros((16, C2), BF)
    for dr in range(4):
        if not any(2 * i + dr in have for i in i_rows):
            continue
        for p in range(3):
            left = jnp.concatenate([c[p, slot(2 * i + dr)] if 2 * i + dr in have else blank for i in i_rows], axis=0)
            got = dot(left, w[p, dr, 256:512])
            total = got if total is None else total + got
    return total


def put(acc, i, got, old=None):
    for h in range(2):
        new = got[:, h * 128 : (h + 1) * 128].reshape(FR, 16, 128)
        acc[h, :, i] = new if old is None else old[h, :, i] + new


def fetch(sources, targets, sems):
    copies = [pltpu.make_async_copy(a, b, sems.at[n]) for n, (a, b) in enumerate(zip(sources, targets, strict=True))]
    for copy in copies:
        copy.start()
    for copy in copies:
        copy.wait()


def early():
    return lax.axis_index("row") % FAR == 0


def first_kernel(feat, k1, proj, send_b, send_a, send_a_too, w, m, strip_sems, k1_in, proj_in, sems):
    last = (lax.axis_index("row") % 2) * (RW - HALO)
    copies = []
    for n, (begin, send) in enumerate([(last, send_b), (RW - HALO - last, send_a), (RW - HALO - last, send_a_too)]):
        copies += [
            pltpu.make_async_copy(feat.at[t, pl.ds(begin, HALO)], send.at[t], strip_sems.at[n, t]) for t in range(FR)
        ]
    for copy in copies:
        copy.start()
    for copy in copies:
        copy.wait()

    @pl.when(early())
    def _():
        fetch((k1, proj), (k1_in, proj_in), sems)
        build_weights(k1_in, proj_in, w, m)


def own_kernel(
    feat, k1, proj, w_in, m_in, w, m, acc, edge, k1_in, proj_in, feat_in, sems, feat_sem, wide, plain, a, b, c, f
):
    copy = pltpu.make_async_copy(feat, feat_in, feat_sem)
    copy.start()

    @pl.when(jnp.logical_not(early()))
    def _():
        fetch((k1, proj), (k1_in, proj_in), sems)
        build_weights(k1_in, proj_in, w, m)

    copy.wait()
    ones = mean_matrix(C1)
    lay_out(lambda t: feat_in[t].reshape(RW * CL, C1), range(RW), ones, wide, plain, a, b, c, f)
    have = range(HALO, HALO + RW)

    def slot(r):
        return r - HALO

    for i in range(6):
        put(acc, i, contribute(i, have, slot, w, m, a, b, f))
    edge[...] = ring(range(6), have, slot, w, c)


def add_side(low, got, w, m, acc_in, edge_in, acc, edge, wide, plain, a, b, c, f):
    lay_out(lambda t: got[t].reshape(HALO * CL, C1), range(HALO), mean_matrix(C1), wide, plain, a, b, c, f)
    whole, part = 5 * low, 1 + 3 * low
    one = 2 * (1 - low)

    def lines(src, p, r):
        return src[p : p + FR, r].reshape(FR * 16, C2)

    blank = jnp.zeros((16, C2), BF)
    total = beside = None
    for p in range(3):
        left = jnp.concatenate(
            [
                jnp.concatenate([lines(src, p, r), blank if src is a else c[p, r]], axis=0)
                for r in range(HALO)
                for src in (a, b)
            ],
            axis=1,
        )
        one_left = jnp.concatenate(
            [jnp.concatenate([lines(src, p, one), blank if src is a else c[p, one]], axis=0) for src in (a, b)], axis=1
        )
        here = dot(left, w[p, pl.ds(low, HALO)].reshape(HALO * 512, C2))
        there = dot(one_left, w[p, 3 * low])
        total = here if total is None else total + here
        beside = there if beside is None else beside + there
    skip = jnp.concatenate([f[:, 1 - low + n].reshape(FR * 16, C2) for n in range(2)], axis=1)
    main = total[0 : FR * 16] + dot(skip, m[...])
    for i, sums, rim in ((whole, main, total), (part, beside[0 : FR * 16], beside)):
        for h in range(2):
            acc[h, :, i] = acc_in[h, :, i] + sums[:, h * 128 : (h + 1) * 128].reshape(FR, 16, 128)
        at = pl.ds(pl.multiple_of(i * 16, 16), 16)
        edge[at] = edge_in[at] + rim[FR * 16 : FR * 16 + 16]


def beside_far():
    return lax.axis_index("row") % FAR < 2


def near_kernel(got, w, m, acc_in, edge_in, acc, edge, *scratch):
    @pl.when(beside_far())
    def _():
        add_side(1 - lax.axis_index("row") % 2, got, w, m, acc_in, edge_in, acc, edge, *scratch)


def far_kernel(got, got_near, w, m, acc_in, edge_in, acc, edge, to_b, to_a, *scratch):
    low = lax.axis_index("row") % 2

    @pl.when(jnp.logical_not(beside_far()))
    def _():
        add_side(1 - low, got_near, w, m, acc_in, edge_in, acc, edge, *scratch)

    add_side(low, got, w, m, acc_in, edge_in, acc, edge, *scratch)
    odd = lax.axis_index("col") % 2 == 1
    flat = acc.reshape(2 * FR * 6 * 16, 128)

    def column(i, j):
        return jnp.concatenate(
            [flat[pl.ds(h * 768 + i * 16 + j, FR, stride=96), :] for h in range(2)], axis=1
        )

    for i in range(6):
        right = jnp.concatenate([column(i, 15), edge[i * 16 + 8 : i * 16 + 16]], axis=0)
        left = jnp.concatenate([edge[i * 16 : i * 16 + 8], column(i, 0)], axis=0)
        to_b[i] = jnp.where(odd, right, left).astype(BF)
        to_a[i] = jnp.where(odd, left, right).astype(BF)


def final_kernel(last_row, last_col, from_b, pair, acc, edge_in, k2, out, lv, edge, wide, a2):
    row, col = lax.axis_index("row"), lax.axis_index("col")
    odd = col % 2 == 1
    for t in range(FR):
        for h in range(2):
            lv[h, t * 96 : (t + 1) * 96] = acc[h, t].reshape(96, 128)
    for i in range(6):
        fb = from_b[i].astype(F32)
        left = jnp.where(odd, pair[0, i].astype(F32), fb)
        right = jnp.where(odd, fb, pair[1, i].astype(F32))
        edge[i * 16 : i * 16 + 8] = edge_in[i * 16 : i * 16 + 8] + left[0:8]
        edge[i * 16 + 8 : i * 16 + 16] = edge_in[i * 16 + 8 : i * 16 + 16] + right[8:16]
        for h in range(2):
            half = slice(h * 128, (h + 1) * 128)
            lv[h, pl.ds(i * 16, FR, stride=96), :] += left[8:16, half]
            lv[h, pl.ds(i * 16 + 15, FR, stride=96), :] += right[0:8, half]
    def level(at, count):
        return jnp.concatenate([lv[0, at : at + count], lv[1, at : at + count]], axis=1)

    ones = mean_matrix(C2)
    keep = [jnp.float32(1.0)] * 6
    keep[0] = jnp.where(row == 0, 0.0, 1.0)
    keep[5] = jnp.where(row == last_row, 0.0, 1.0)
    keep_left = jnp.where(col == 0, 0.0, 1.0)
    keep_right = jnp.where(col == last_col, 0.0, 1.0)
    for t in range(FR):
        act = normed_silu(level(t * 96, 96), ones)
        for i in range(6):
            base = (t * 6 + i) * 32 + 8
            kept = act[i * 16 : (i + 1) * 16] * keep[i]
            for h in range(2):
                wide[h, base : base + 16] = kept[:, h * 128 : (h + 1) * 128]
    act = normed_silu(edge[...], ones)
    for i in range(6):
        for h in range(2):
            half = slice(h * 128, (h + 1) * 128)
            wide[h, pl.ds(i * 32 + 7, FR, stride=192), :] = act[i * 16 : i * 16 + 8, half] * (keep[i] * keep_left)
            wide[h, pl.ds(i * 32 + 24, FR, stride=192), :] = act[i * 16 + 8 : i * 16 + 16, half] * (
                keep[i] * keep_right
            )
    for s in range(3):
        for i in range(6):
            for t in range(2):
                a2[s, t, i] = jnp.zeros((16, C2), BF)
            for t in range(FR):
                base = (t * 6 + i) * 32 + 7 + s
                for h in range(2):
                    a2[s, t + 2, i, :, h * 128 : (h + 1) * 128] = wide[h, base : base + 16].astype(BF)
    for i in range(4):
        total = None
        for p in range(3):
            left = jnp.concatenate(
                [a2[s, p : p + FR, i + q].reshape(FR * 16, C2) for q in range(3) for s in range(3)], axis=1
            )
            got = dot(left, k2[p].reshape(9 * C2, C2))
            total = got if total is None else total + got
        for t in range(FR):
            at = (t * 6 + i + 1) * 16
            out[t, i] = (level(at, 16) + total[t * 16 : (t + 1) * 16]).astype(BF)


def in_vmem(shape, dtype):
    return jax.ShapeDtypeStruct(shape, dtype)


def operands(rows):
    return [
        pltpu.VMEM(((FR + 2) * rows * PITCH, C1), F32),
        pltpu.VMEM((FR * rows * CL, C1), F32),
        pltpu.VMEM((FR + 2, rows, 16, C2), BF),
        pltpu.VMEM((FR + 2, rows, 16, C2), BF),
        pltpu.VMEM((3, rows, 16, C2), BF),
        pltpu.VMEM((FR, rows, 16, C2), BF),
    ]


ROWS_SHAPE = in_vmem((FR, HALO, CL, C1), BF)
W_SHAPE = in_vmem((3, 4, 512, C2), BF)
M_SHAPE = in_vmem((512, C2), BF)
ACC_SHAPE = in_vmem((2, FR, 6, 16, 128), F32)
EDGE_SHAPE = in_vmem((96, C2), F32)
STRIP_SHAPE = in_vmem((6, 16, C2), BF)
PARAMS = pltpu.CompilerParams(vmem_limit_bytes=24 * 2**20)


def in_hbm(x):
    return pltpu.with_memory_space_constraint(x, pltpu.HBM)


def weight_scratch():
    return [
        pltpu.VMEM((3, 3, 3, C1, C1), BF),
        pltpu.VMEM((4 * C1, C2), BF),
    ]


def first_part(feat, k1, proj):
    return pl.pallas_call(
        first_kernel,
        out_shape=(ROWS_SHAPE,) * 3 + (W_SHAPE, M_SHAPE),
        in_specs=[HBM] * 3,
        out_specs=(VM,) * 5,
        scratch_shapes=[pltpu.SemaphoreType.DMA((3, FR))] + weight_scratch() + [pltpu.SemaphoreType.DMA((2,))],
        compiler_params=PARAMS,
        name="first_part",
    )(in_hbm(feat), in_hbm(k1), in_hbm(proj))


def own_part(feat, k1, proj, w, m):
    return pl.pallas_call(
        own_kernel,
        out_shape=(W_SHAPE, M_SHAPE, ACC_SHAPE, EDGE_SHAPE),
        in_specs=[HBM] * 3 + [VM] * 2,
        out_specs=(VM,) * 4,
        scratch_shapes=weight_scratch()
        + [pltpu.VMEM((FR, RW, CL, C1), BF), pltpu.SemaphoreType.DMA((2,)), pltpu.SemaphoreType.DMA]
        + operands(RW),
        input_output_aliases={3: 0, 4: 1},
        compiler_params=PARAMS,
        name="own_part",
    )(in_hbm(feat), in_hbm(k1), in_hbm(proj), w, m)


def near_part(got, w, m, acc, edge):
    return pl.pallas_call(
        near_kernel,
        out_shape=(ACC_SHAPE, EDGE_SHAPE),
        in_specs=[VM] * 5,
        out_specs=(VM,) * 2,
        scratch_shapes=operands(HALO),
        input_output_aliases={3: 0, 4: 1},
        compiler_params=PARAMS,
        name="near_part",
    )(got, w, m, acc, edge)


def far_part(got, got_near, w, m, acc, edge):
    return pl.pallas_call(
        far_kernel,
        out_shape=(ACC_SHAPE, EDGE_SHAPE, STRIP_SHAPE, STRIP_SHAPE),
        in_specs=[VM] * 6,
        out_specs=(VM,) * 4,
        scratch_shapes=operands(HALO),
        input_output_aliases={4: 0, 5: 1},
        compiler_params=PARAMS,
        name="far_part",
    )(got, got_near, w, m, acc, edge)


def final_part(last_row, last_col, from_b, pair, acc, edge, k2):
    def kernel(*refs):
        final_kernel(last_row, last_col, *refs)

    return pl.pallas_call(
        kernel,
        out_shape=in_vmem((FR, 4, 16, C2), BF),
        in_specs=[VM] * 5,
        out_specs=VM,
        scratch_shapes=[
            pltpu.VMEM((2, FR * 6 * 16, 128), F32),
            pltpu.VMEM((96, C2), F32),
            pltpu.VMEM((2, FR * 6 * 32, 128), F32),
            pltpu.VMEM((3, FR + 2, 6, 16, C2), BF),
        ],
        compiler_params=PARAMS,
        name="final_part",
    )(from_b, pair, acc, edge, k2)


def pairs(first, count):
    swaps = []
    for i in range(first, count - 1, 2):
        swaps += [(i, i + 1), (i + 1, i)]
    return swaps


def local(features, kernel_one, projection, kernel_two):
    rows, cols = lax.axis_size("row"), lax.axis_size("col")
    send_b, send_a, send_a_too, w, m = first_part(features, kernel_one, projection)
    far_side = [(i, j) for i, j in pairs(0, rows) if min(i, j) % FAR == 0]
    others = [pair for pair in pairs(0, rows) if pair not in far_side]
    from_a = lax.ppermute(send_a, "row", far_side)
    from_b = lax.ppermute(send_b, "row", pairs(1, rows))
    from_a_too = lax.ppermute(send_a_too, "row", others)
    w, m, acc, edge = own_part(features, kernel_one, projection, w, m)
    acc, edge = near_part(from_a, w, m, acc, edge)
    acc, edge, to_b, to_a = far_part(from_b, from_a_too, w, m, acc, edge)
    from_b = lax.ppermute(to_b, "col", pairs(1, cols))
    pair = lax.all_gather(to_a, "col", axis_index_groups=[[i, i + 1] for i in range(0, cols, 2)])
    return final_part(rows - 1, cols - 1, from_b, pair, acc, edge, kernel_two)


def solution(mesh):
    return jax.shard_map(
        local,
        mesh=mesh,
        in_specs=(P(None, "row", "col", None), P(), P(), P()),
        out_specs=P(None, "row", "col", None),
        check_vma=False,
    )
```

```python
import jax
import jax.numpy as jnp
from jax import lax
from jax.experimental import pallas as pl
from jax.experimental.pallas import tpu as pltpu
from jax.sharding import PartitionSpec as P

NORM_EPS = 1e-06
FR, RW, CL, C1, C2 = 8, 8, 32, 128, 256
HALO = 3
BF, F32 = jnp.bfloat16, jnp.float32
PITCH = 48
COLS_OF = (1, 2, 0, 3)
FAR = 16
VM = pl.BlockSpec(memory_space=pltpu.VMEM)
HBM = pl.BlockSpec(memory_space=pltpu.HBM)


def dot(a, b):
    return jnp.dot(a, b, preferred_element_type=F32)


def normed_silu(x, ones):
    mean = dot((x * x).astype(BF), ones)
    half = x * (0.5 * lax.rsqrt(mean + NORM_EPS))
    return half + half * jnp.tanh(half)


def mean_matrix(n):
    return jnp.full((n, n), 1.0 / n, BF)


def build_weights(k1, proj, w, m):
    p0, p1, p2, p3 = (proj[i * C1 : (i + 1) * C1].astype(F32) * 0.5 for i in range(4))
    row = lax.broadcasted_iota(jnp.int32, (C1, C2), 0)
    col = lax.broadcasted_iota(jnp.int32, (C1, C2), 1)
    twice = jnp.where((col == row) | (col == row + C1), 0.5, 0.0).astype(F32)
    m[0:C1] = (p0 + p1 + p2 + p3 + twice).astype(BF)
    m[C1 : 2 * C1] = (p0 + p1 - p2 - p3 + twice).astype(BF)
    m[2 * C1 : 3 * C1] = (p0 - p1 + p2 - p3 + twice).astype(BF)
    m[3 * C1 : 4 * C1] = (p0 - p1 - p2 + p3 + twice).astype(BF)
    zero = jnp.zeros((C1, C1), BF)

    def tap(p, q, s):
        return k1[p, q, s] if 0 <= s < 3 else zero

    for p in range(3):
        for dr in range(4):
            pairs = [pr for pr in range(2) if 0 <= dr - pr < 3]
            left = jnp.concatenate(
                [
                    jnp.concatenate([tap(p, dr - pr, dc - pc) for pr in pairs for pc in range(2)], axis=1)
                    for dc in COLS_OF
                ],
                axis=0,
            )
            w[p, dr] = dot(left, m[pairs[0] * 256 : (pairs[-1] + 1) * 256]).astype(BF)


def lay_out(feature, row_of, ones, wide, plain, a, b, c, f):
    rows = len(row_of)
    span = rows * PITCH
    for t in range(2):
        for r, at in enumerate(row_of):
            base = t * span + r * PITCH
            wide[base + 8 : base + 16] = jnp.zeros((8, C1), F32)
            wide[base + 32 : base + 40] = jnp.zeros((8, C1), F32)
            a[t, at] = jnp.zeros((16, C2), BF)
            b[t, at] = jnp.zeros((16, C2), BF)
    for t in range(FR):
        x = feature(t).astype(F32)
        act = normed_silu(x, ones)
        for r, at in enumerate(row_of):
            base = (t + 2) * span + r * PITCH
            wide[base : base + 8] = jnp.zeros((8, C1), F32)
            wide[base + 40 : base + 48] = jnp.zeros((8, C1), F32)
            wide[base + 8 : base + 40] = act[r * CL : (r + 1) * CL]
            own = (t * rows + r) * CL
            plain[own : own + CL] = x[r * CL : (r + 1) * CL]
            a[t + 2, at, :, 0:C1] = wide[pl.ds(base + 8, 16, stride=2), :].astype(BF)
            a[t + 2, at, :, C1:C2] = wide[pl.ds(base + 9, 16, stride=2), :].astype(BF)
            b[t + 2, at, :, 0:C1] = wide[pl.ds(base + 7, 16, stride=2), :].astype(BF)
            b[t + 2, at, :, C1:C2] = wide[pl.ds(base + 10, 16, stride=2), :].astype(BF)
            f[t, at, :, 0:C1] = plain[pl.ds(own, 16, stride=2), :].astype(BF)
            f[t, at, :, C1:C2] = plain[pl.ds(own + 1, 16, stride=2), :].astype(BF)
    zero = jnp.zeros((FR, C1), F32)
    for p in range(3):
        for r, at in enumerate(row_of):
            base = p * span + r * PITCH + 8
            first = wide[pl.ds(base, FR, stride=span), :]
            last = wide[pl.ds(base + CL - 1, FR, stride=span), :]
            c[p, at, :, 0:C1] = jnp.concatenate([zero, last], axis=0).astype(BF)
            c[p, at, :, C1:C2] = jnp.concatenate([first, zero], axis=0).astype(BF)


def contribute(i, have, slot, w, m, a, b, f):
    total = None
    taps = [dr for dr in range(4) if 2 * i + dr in have]
    for p in range(3):
        left = jnp.concatenate(
            [src[p : p + FR, slot(2 * i + dr)].reshape(FR * 16, C2) for dr in taps for src in (a, b)], axis=1
        )
        right = w[p, taps[0] : taps[-1] + 1].reshape(len(taps) * 512, C2)
        got = dot(left, right)
        total = got if total is None else total + got
    for pr in range(2):
        if 2 * i + 1 + pr in have:
            total = total + dot(f[:, slot(2 * i + 1 + pr)].reshape(FR * 16, C2), m[pr * 256 : (pr + 1) * 256])
    return total


def ring(i_rows, have, slot, w, c):
    total = None
    blank = jnp.zeros((16, C2), BF)
    for dr in range(4):
        if not any(2 * i + dr in have for i in i_rows):
            continue
        for p in range(3):
            left = jnp.concatenate([c[p, slot(2 * i + dr)] if 2 * i + dr in have else blank for i in i_rows], axis=0)
            got = dot(left, w[p, dr, 256:512])
            total = got if total is None else total + got
    return total


def put(acc, i, got, old=None):
    for h in range(2):
        new = got[:, h * 128 : (h + 1) * 128].reshape(FR, 16, 128)
        acc[h, :, i] = new if old is None else old[h, :, i] + new


def fetch(sources, targets, sems):
    copies = [pltpu.make_async_copy(a, b, sems.at[n]) for n, (a, b) in enumerate(zip(sources, targets, strict=True))]
    for copy in copies:
        copy.start()
    for copy in copies:
        copy.wait()


def early():
    return lax.axis_index("row") % FAR == 0


def first_kernel(feat, k1, proj, send_b, send_a, send_a_too, w, m, strip_sems, k1_in, proj_in, sems):
    last = (lax.axis_index("row") % 2) * (RW - HALO)

    def strips(n, begin, send):
        return [
            pltpu.make_async_copy(feat.at[t, pl.ds(begin, HALO)], send.at[t], strip_sems.at[n, t]) for t in range(FR)
        ]

    far = strips(0, last, send_b)
    for copy in far:
        copy.start()
    for wanted, send in ((beside_far(), send_a), (jnp.logical_not(beside_far()), send_a_too)):

        @pl.when(wanted)
        def _(send=send):
            near = strips(1, RW - HALO - last, send)
            for copy in near:
                copy.start()
            for copy in near:
                copy.wait()

    for copy in far:
        copy.wait()

    @pl.when(early())
    def _():
        fetch((k1, proj), (k1_in, proj_in), sems)
        build_weights(k1_in, proj_in, w, m)


def own_kernel(
    feat, k1, proj, w_in, m_in, w, m, acc, edge, k1_in, proj_in, feat_in, sems, feat_sem, wide, plain, a, b, c, f
):
    copy = pltpu.make_async_copy(feat, feat_in, feat_sem)
    copy.start()

    @pl.when(jnp.logical_not(early()))
    def _():
        fetch((k1, proj), (k1_in, proj_in), sems)
        build_weights(k1_in, proj_in, w, m)

    copy.wait()
    ones = mean_matrix(C1)
    lay_out(lambda t: feat_in[t].reshape(RW * CL, C1), range(RW), ones, wide, plain, a, b, c, f)
    have = range(HALO, HALO + RW)

    def slot(r):
        return r - HALO

    for i in range(6):
        put(acc, i, contribute(i, have, slot, w, m, a, b, f))
    edge[...] = ring(range(6), have, slot, w, c)


def add_side(low, got, w, m, acc_in, edge_in, acc, edge, wide, plain, a, b, c, f):
    lay_out(lambda t: got[t].reshape(HALO * CL, C1), range(HALO), mean_matrix(C1), wide, plain, a, b, c, f)
    whole, part = 5 * low, 1 + 3 * low
    one = 2 * (1 - low)

    def lines(src, p, r):
        return src[p : p + FR, r].reshape(FR * 16, C2)

    blank = jnp.zeros((16, C2), BF)
    total = beside = None
    for p in range(3):
        left = jnp.concatenate(
            [
                jnp.concatenate([lines(src, p, r), blank if src is a else c[p, r]], axis=0)
                for r in range(HALO)
                for src in (a, b)
            ],
            axis=1,
        )
        one_left = jnp.concatenate(
            [jnp.concatenate([lines(src, p, one), blank if src is a else c[p, one]], axis=0) for src in (a, b)], axis=1
        )
        here = dot(left, w[p, pl.ds(low, HALO)].reshape(HALO * 512, C2))
        there = dot(one_left, w[p, 3 * low])
        total = here if total is None else total + here
        beside = there if beside is None else beside + there
    skip = jnp.concatenate([f[:, 1 - low + n].reshape(FR * 16, C2) for n in range(2)], axis=1)
    main = total[0 : FR * 16] + dot(skip, m[...])
    for i, sums, rim in ((whole, main, total), (part, beside[0 : FR * 16], beside)):
        for h in range(2):
            acc[h, :, i] = acc_in[h, :, i] + sums[:, h * 128 : (h + 1) * 128].reshape(FR, 16, 128)
        at = pl.ds(pl.multiple_of(i * 16, 16), 16)
        edge[at] = edge_in[at] + rim[FR * 16 : FR * 16 + 16]


def beside_far():
    return lax.axis_index("row") % FAR < 2


def near_kernel(got, w, m, acc_in, edge_in, acc, edge, *scratch):
    @pl.when(beside_far())
    def _():
        add_side(1 - lax.axis_index("row") % 2, got, w, m, acc_in, edge_in, acc, edge, *scratch)


def far_kernel(got, got_near, w, m, acc_in, edge_in, acc, edge, to_b, to_a, *scratch):
    low = lax.axis_index("row") % 2

    @pl.when(jnp.logical_not(beside_far()))
    def _():
        add_side(1 - low, got_near, w, m, acc_in, edge_in, acc, edge, *scratch)

    add_side(low, got, w, m, acc_in, edge_in, acc, edge, *scratch)
    odd = lax.axis_index("col") % 2 == 1
    flat = acc.reshape(2 * FR * 6 * 16, 128)

    def column(i, j):
        return jnp.concatenate(
            [flat[pl.ds(h * 768 + i * 16 + j, FR, stride=96), :] for h in range(2)], axis=1
        )

    for i in range(6):
        right = jnp.concatenate([column(i, 15), edge[i * 16 + 8 : i * 16 + 16]], axis=0)
        left = jnp.concatenate([edge[i * 16 : i * 16 + 8], column(i, 0)], axis=0)
        to_b[i] = jnp.where(odd, right, left).astype(BF)
        to_a[i] = jnp.where(odd, left, right).astype(BF)


def final_kernel(last_row, last_col, from_b, pair, acc, edge_in, k2, out, lv, edge, wide, a2):
    row, col = lax.axis_index("row"), lax.axis_index("col")
    odd = col % 2 == 1
    for t in range(FR):
        for h in range(2):
            lv[h, t * 96 : (t + 1) * 96] = acc[h, t].reshape(96, 128)
    for i in range(6):
        fb = from_b[i].astype(F32)
        left = jnp.where(odd, pair[0, i].astype(F32), fb)
        right = jnp.where(odd, fb, pair[1, i].astype(F32))
        edge[i * 16 : i * 16 + 8] = edge_in[i * 16 : i * 16 + 8] + left[0:8]
        edge[i * 16 + 8 : i * 16 + 16] = edge_in[i * 16 + 8 : i * 16 + 16] + right[8:16]
        for h in range(2):
            half = slice(h * 128, (h + 1) * 128)
            lv[h, pl.ds(i * 16, FR, stride=96), :] += left[8:16, half]
            lv[h, pl.ds(i * 16 + 15, FR, stride=96), :] += right[0:8, half]
    def level(at, count):
        return jnp.concatenate([lv[0, at : at + count], lv[1, at : at + count]], axis=1)

    ones = mean_matrix(C2)
    keep = [jnp.float32(1.0)] * 6
    keep[0] = jnp.where(row == 0, 0.0, 1.0)
    keep[5] = jnp.where(row == last_row, 0.0, 1.0)
    keep_left = jnp.where(col == 0, 0.0, 1.0)
    keep_right = jnp.where(col == last_col, 0.0, 1.0)
    for t in range(FR):
        act = normed_silu(level(t * 96, 96), ones)
        for i in range(6):
            base = (t * 6 + i) * 32 + 8
            kept = act[i * 16 : (i + 1) * 16] * keep[i]
            for h in range(2):
                wide[h, base : base + 16] = kept[:, h * 128 : (h + 1) * 128]
    act = normed_silu(edge[...], ones)
    for i in range(6):
        for h in range(2):
            half = slice(h * 128, (h + 1) * 128)
            wide[h, pl.ds(i * 32 + 7, FR, stride=192), :] = act[i * 16 : i * 16 + 8, half] * (keep[i] * keep_left)
            wide[h, pl.ds(i * 32 + 24, FR, stride=192), :] = act[i * 16 + 8 : i * 16 + 16, half] * (
                keep[i] * keep_right
            )
    for s in range(3):
        for i in range(6):
            for t in range(2):
                a2[s, t, i] = jnp.zeros((16, C2), BF)
            for t in range(FR):
                base = (t * 6 + i) * 32 + 7 + s
                for h in range(2):
                    a2[s, t + 2, i, :, h * 128 : (h + 1) * 128] = wide[h, base : base + 16].astype(BF)
    for i in range(4):
        total = None
        for p in range(3):
            left = jnp.concatenate(
                [a2[s, p : p + FR, i + q].reshape(FR * 16, C2) for q in range(3) for s in range(3)], axis=1
            )
            got = dot(left, k2[p].reshape(9 * C2, C2))
            total = got if total is None else total + got
        for t in range(FR):
            at = (t * 6 + i + 1) * 16
            out[t, i] = (level(at, 16) + total[t * 16 : (t + 1) * 16]).astype(BF)


def in_vmem(shape, dtype):
    return jax.ShapeDtypeStruct(shape, dtype)


def operands(rows):
    return [
        pltpu.VMEM(((FR + 2) * rows * PITCH, C1), F32),
        pltpu.VMEM((FR * rows * CL, C1), F32),
        pltpu.VMEM((FR + 2, rows, 16, C2), BF),
        pltpu.VMEM((FR + 2, rows, 16, C2), BF),
        pltpu.VMEM((3, rows, 16, C2), BF),
        pltpu.VMEM((FR, rows, 16, C2), BF),
    ]


ROWS_SHAPE = in_vmem((FR, HALO, CL, C1), BF)
W_SHAPE = in_vmem((3, 4, 512, C2), BF)
M_SHAPE = in_vmem((512, C2), BF)
ACC_SHAPE = in_vmem((2, FR, 6, 16, 128), F32)
EDGE_SHAPE = in_vmem((96, C2), F32)
STRIP_SHAPE = in_vmem((6, 16, C2), BF)
PARAMS = pltpu.CompilerParams(vmem_limit_bytes=24 * 2**20)


def in_hbm(x):
    return pltpu.with_memory_space_constraint(x, pltpu.HBM)


def weight_scratch():
    return [
        pltpu.VMEM((3, 3, 3, C1, C1), BF),
        pltpu.VMEM((4 * C1, C2), BF),
    ]


def first_part(feat, k1, proj):
    return pl.pallas_call(
        first_kernel,
        out_shape=(ROWS_SHAPE,) * 3 + (W_SHAPE, M_SHAPE),
        in_specs=[HBM] * 3,
        out_specs=(VM,) * 5,
        scratch_shapes=[pltpu.SemaphoreType.DMA((2, FR))] + weight_scratch() + [pltpu.SemaphoreType.DMA((2,))],
        compiler_params=PARAMS,
        name="first_part",
    )(in_hbm(feat), in_hbm(k1), in_hbm(proj))


def own_part(feat, k1, proj, w, m):
    return pl.pallas_call(
        own_kernel,
        out_shape=(W_SHAPE, M_SHAPE, ACC_SHAPE, EDGE_SHAPE),
        in_specs=[HBM] * 3 + [VM] * 2,
        out_specs=(VM,) * 4,
        scratch_shapes=weight_scratch()
        + [pltpu.VMEM((FR, RW, CL, C1), BF), pltpu.SemaphoreType.DMA((2,)), pltpu.SemaphoreType.DMA]
        + operands(RW),
        input_output_aliases={3: 0, 4: 1},
        compiler_params=PARAMS,
        name="own_part",
    )(in_hbm(feat), in_hbm(k1), in_hbm(proj), w, m)


def near_part(got, w, m, acc, edge):
    return pl.pallas_call(
        near_kernel,
        out_shape=(ACC_SHAPE, EDGE_SHAPE),
        in_specs=[VM] * 5,
        out_specs=(VM,) * 2,
        scratch_shapes=operands(HALO),
        input_output_aliases={3: 0, 4: 1},
        compiler_params=PARAMS,
        name="near_part",
    )(got, w, m, acc, edge)


def far_part(got, got_near, w, m, acc, edge):
    return pl.pallas_call(
        far_kernel,
        out_shape=(ACC_SHAPE, EDGE_SHAPE, STRIP_SHAPE, STRIP_SHAPE),
        in_specs=[VM] * 6,
        out_specs=(VM,) * 4,
        scratch_shapes=operands(HALO),
        input_output_aliases={4: 0, 5: 1},
        compiler_params=PARAMS,
        name="far_part",
    )(got, got_near, w, m, acc, edge)


def final_part(last_row, last_col, from_b, pair, acc, edge, k2):
    def kernel(*refs):
        final_kernel(last_row, last_col, *refs)

    return pl.pallas_call(
        kernel,
        out_shape=in_vmem((FR, 4, 16, C2), BF),
        in_specs=[VM] * 5,
        out_specs=VM,
        scratch_shapes=[
            pltpu.VMEM((2, FR * 6 * 16, 128), F32),
            pltpu.VMEM((96, C2), F32),
            pltpu.VMEM((2, FR * 6 * 32, 128), F32),
            pltpu.VMEM((3, FR + 2, 6, 16, C2), BF),
        ],
        compiler_params=PARAMS,
        name="final_part",
    )(from_b, pair, acc, edge, k2)


def pairs(first, count):
    swaps = []
    for i in range(first, count - 1, 2):
        swaps += [(i, i + 1), (i + 1, i)]
    return swaps


def local(features, kernel_one, projection, kernel_two):
    rows, cols = lax.axis_size("row"), lax.axis_size("col")
    send_b, send_a, send_a_too, w, m = first_part(features, kernel_one, projection)
    far_side = [(i, j) for i, j in pairs(0, rows) if min(i, j) % FAR == 0]
    others = [pair for pair in pairs(0, rows) if pair not in far_side]
    from_a = lax.ppermute(send_a, "row", far_side)
    from_b = lax.ppermute(send_b, "row", pairs(1, rows))
    from_a_too = lax.ppermute(send_a_too, "row", others)
    w, m, acc, edge = own_part(features, kernel_one, projection, w, m)
    acc, edge = near_part(from_a, w, m, acc, edge)
    acc, edge, to_b, to_a = far_part(from_b, from_a_too, w, m, acc, edge)
    from_b = lax.ppermute(to_b, "col", pairs(1, cols))
    pair = lax.all_gather(to_a, "col", axis_index_groups=[[i, i + 1] for i in range(0, cols, 2)])
    return final_part(rows - 1, cols - 1, from_b, pair, acc, edge, kernel_two)


def solution(mesh):
    return jax.shard_map(
        local,
        mesh=mesh,
        in_specs=(P(None, "row", "col", None), P(), P(), P()),
        out_specs=P(None, "row", "col", None),
        check_vma=False,
    )
```

```python
import jax
import jax.numpy as jnp
from jax import lax
from jax.experimental import pallas as pl
from jax.experimental.pallas import tpu as pltpu
from jax.sharding import PartitionSpec as P

NORM_EPS = 1e-06
FR, RW, CL, C1, C2 = 8, 8, 32, 128, 256
HALO = 3
BF, F32 = jnp.bfloat16, jnp.float32
PITCH = 48
COLS_OF = (1, 2, 0, 3)
NEXT = 8
FAR = 16
VM = pl.BlockSpec(memory_space=pltpu.VMEM)
HBM = pl.BlockSpec(memory_space=pltpu.HBM)


def dot(a, b):
    return jnp.dot(a, b, preferred_element_type=F32)


def normed_silu(x, ones):
    mean = dot((x * x).astype(BF), ones)
    half = x * (0.5 * lax.rsqrt(mean + NORM_EPS))
    return half + half * jnp.tanh(half)


def mean_matrix(n):
    return jnp.full((n, n), 1.0 / n, BF)


def build_maps(proj, m):
    p0, p1, p2, p3 = (proj[i * C1 : (i + 1) * C1].astype(F32) * 0.5 for i in range(4))
    row = lax.broadcasted_iota(jnp.int32, (C1, C2), 0)
    col = lax.broadcasted_iota(jnp.int32, (C1, C2), 1)
    twice = jnp.where((col == row) | (col == row + C1), 0.5, 0.0).astype(F32)
    m[0:C1] = (p0 + p1 + p2 + p3 + twice).astype(BF)
    m[C1 : 2 * C1] = (p0 + p1 - p2 - p3 + twice).astype(BF)
    m[2 * C1 : 3 * C1] = (p0 - p1 + p2 - p3 + twice).astype(BF)
    m[3 * C1 : 4 * C1] = (p0 - p1 - p2 + p3 + twice).astype(BF)


def build_weights(frames, k1, w, m):
    zero = jnp.zeros((C1, C1), BF)

    def tap(p, q, s):
        return k1[p, q, s] if 0 <= s < 3 else zero

    for p in frames:
        for dr in range(4):
            pairs = [pr for pr in range(2) if 0 <= dr - pr < 3]
            left = jnp.concatenate(
                [
                    jnp.concatenate([tap(p, dr - pr, dc - pc) for pr in pairs for pc in range(2)], axis=1)
                    for dc in COLS_OF
                ],
                axis=0,
            )
            w[p, dr] = dot(left, m[pairs[0] * 256 : (pairs[-1] + 1) * 256]).astype(BF)


def lay_out(feature, row_of, ones, wide, plain, a, b, c, f):
    rows = len(row_of)
    span = rows * PITCH
    for t in range(2):
        for r, at in enumerate(row_of):
            base = t * span + r * PITCH
            wide[base + 8 : base + 16] = jnp.zeros((8, C1), F32)
            wide[base + 32 : base + 40] = jnp.zeros((8, C1), F32)
            a[t, at] = jnp.zeros((16, C2), BF)
            b[t, at] = jnp.zeros((16, C2), BF)
    for t in range(FR):
        x = feature(t).astype(F32)
        act = normed_silu(x, ones)
        for r, at in enumerate(row_of):
            base = (t + 2) * span + r * PITCH
            wide[base : base + 8] = jnp.zeros((8, C1), F32)
            wide[base + 40 : base + 48] = jnp.zeros((8, C1), F32)
            wide[base + 8 : base + 40] = act[r * CL : (r + 1) * CL]
            own = (t * rows + r) * CL
            plain[own : own + CL] = x[r * CL : (r + 1) * CL]
            a[t + 2, at, :, 0:C1] = wide[pl.ds(base + 8, 16, stride=2), :].astype(BF)
            a[t + 2, at, :, C1:C2] = wide[pl.ds(base + 9, 16, stride=2), :].astype(BF)
            b[t + 2, at, :, 0:C1] = wide[pl.ds(base + 7, 16, stride=2), :].astype(BF)
            b[t + 2, at, :, C1:C2] = wide[pl.ds(base + 10, 16, stride=2), :].astype(BF)
            f[t, at, :, 0:C1] = plain[pl.ds(own, 16, stride=2), :].astype(BF)
            f[t, at, :, C1:C2] = plain[pl.ds(own + 1, 16, stride=2), :].astype(BF)
    zero = jnp.zeros((FR, C1), F32)
    for p in range(3):
        for r, at in enumerate(row_of):
            base = p * span + r * PITCH + 8
            first = wide[pl.ds(base, FR, stride=span), :]
            last = wide[pl.ds(base + CL - 1, FR, stride=span), :]
            c[p, at, :, 0:C1] = jnp.concatenate([zero, last], axis=0).astype(BF)
            c[p, at, :, C1:C2] = jnp.concatenate([first, zero], axis=0).astype(BF)


def contribute(i, have, slot, w, m, a, b, f):
    total = None
    taps = [dr for dr in range(4) if 2 * i + dr in have]
    for p in range(3):
        left = jnp.concatenate(
            [src[p : p + FR, slot(2 * i + dr)].reshape(FR * 16, C2) for dr in taps for src in (a, b)], axis=1
        )
        right = w[p, taps[0] : taps[-1] + 1].reshape(len(taps) * 512, C2)
        got = dot(left, right)
        total = got if total is None else total + got
    for pr in range(2):
        if 2 * i + 1 + pr in have:
            total = total + dot(f[:, slot(2 * i + 1 + pr)].reshape(FR * 16, C2), m[pr * 256 : (pr + 1) * 256])
    return total


def ring(i_rows, have, slot, w, c):
    total = None
    blank = jnp.zeros((16, C2), BF)
    for dr in range(4):
        if not any(2 * i + dr in have for i in i_rows):
            continue
        for p in range(3):
            left = jnp.concatenate([c[p, slot(2 * i + dr)] if 2 * i + dr in have else blank for i in i_rows], axis=0)
            got = dot(left, w[p, dr, 256:512])
            total = got if total is None else total + got
    return total


def put(acc, i, got, old=None):
    for h in range(2):
        new = got[:, h * 128 : (h + 1) * 128].reshape(FR, 16, 128)
        acc[h, :, i] = new if old is None else old[h, :, i] + new


def early():
    return lax.axis_index("row") % FAR == 0


def waits():
    return lax.axis_index("row") % NEXT == 0


def first_kernel(
    feat, k1, proj, send_b, send_a, send_a_too, w, m, feat_in, k1_in, strip_sems, feat_sem, proj_in, sems
):
    last = (lax.axis_index("row") % 2) * (RW - HALO)

    def strips(n, begin, send):
        return [
            pltpu.make_async_copy(feat.at[t, pl.ds(begin, HALO)], send.at[t], strip_sems.at[n, t]) for t in range(FR)
        ]

    far = strips(0, last, send_b)
    for copy in far:
        copy.start()

    @pl.when(waits())
    def _():
        pltpu.make_async_copy(feat, feat_in, feat_sem).start()

    weights = [pltpu.make_async_copy(x, y, sems.at[n]) for n, (x, y) in enumerate([(k1, k1_in), (proj, proj_in)])]

    @pl.when(early())
    def _():
        for copy in weights:
            copy.start()

    for wanted, send in ((beside_far(), send_a), (jnp.logical_not(beside_far()), send_a_too)):

        @pl.when(wanted)
        def _(send=send):
            near = strips(1, RW - HALO - last, send)
            for copy in near:
                copy.start()
            for copy in near:
                copy.wait()

    for copy in far:
        copy.wait()

    @pl.when(waits())
    def _():
        pltpu.make_async_copy(feat, feat_in, feat_sem).wait()

    @pl.when(early())
    def _():
        for copy in weights:
            copy.wait()
        build_maps(proj_in, m)
        build_weights((0,), k1_in, w, m)


def middle_columns(acc, tall, act_in):
    x = jnp.concatenate([acc[h, :, 2:4].reshape(FR * 2 * 16, 128) for h in range(2)], axis=1)
    column = lax.broadcasted_iota(jnp.int32, (FR * 2 * 16, C2), 0) % 16
    inner = jnp.where((column > 0) & (column < 15), 1.0, 0.0).astype(F32)
    act = normed_silu(x, mean_matrix(C2)) * inner
    for n in range(2 * FR):
        for h in range(2):
            tall[h, n * 32 : n * 32 + 8] = jnp.zeros((8, 128), F32)
            tall[h, n * 32 + 24 : n * 32 + 32] = jnp.zeros((8, 128), F32)
            tall[h, n * 32 + 8 : n * 32 + 24] = act[n * 16 : (n + 1) * 16, h * 128 : (h + 1) * 128]
    for s in range(3):
        for n in range(2):
            for t in range(2):
                act_in[s, t, n] = jnp.zeros((16, C2), BF)
            for t in range(FR):
                base = (t * 2 + n) * 32 + 7 + s
                for h in range(2):
                    act_in[s, t + 2, n, :, h * 128 : (h + 1) * 128] = tall[h, base : base + 16].astype(BF)


def middle(k2, mid, act_in):
    for i in range(4):
        taps = [q for q in range(3) if i + q in (2, 3)]
        total = None
        for p in range(3):
            left = jnp.concatenate(
                [act_in[s, p : p + FR, i + q - 2].reshape(FR * 16, C2) for q in taps for s in range(3)], axis=1
            )
            got = dot(left, k2[p, taps[0] : taps[-1] + 1].reshape(len(taps) * 3 * C2, C2))
            total = got if total is None else total + got
        for h in range(2):
            mid[h, i * FR * 16 : (i + 1) * FR * 16] = total[:, h * 128 : (h + 1) * 128]


def own_kernel(
    feat, k1, proj, k2_far, w_in, m_in, feat_here, k1_here,
    w, m, feat_in, k1_in, acc, edge, k2, mid,
    proj_in, sems, late_sems, tall, act_in, wide, plain, a, b, c, f,
):
    copy = pltpu.make_async_copy(feat, feat_in, late_sems.at[0])

    @pl.when(jnp.logical_not(waits()))
    def _():
        copy.start()

    make = jnp.logical_not(early())
    sources = [
        pltpu.make_async_copy(x, y, sems.at[n]) for n, (x, y) in enumerate([(k1, k1_in), (proj, proj_in)])
    ]

    @pl.when(make)
    def _():
        for source in sources:
            source.start()

    @pl.when(jnp.logical_not(waits()))
    def _():
        copy.wait()

    @pl.when(make)
    def _():
        for source in sources:
            source.wait()

    copy_k2 = pltpu.make_async_copy(k2_far, k2, late_sems.at[1])
    copy_k2.start()

    @pl.when(make)
    def _():
        build_maps(proj_in, m)
        build_weights((0,), k1_in, w, m)

    build_weights((1, 2), k1_in, w, m)
    ones = mean_matrix(C1)
    lay_out(lambda t: feat_in[t].reshape(RW * CL, C1), range(RW), ones, wide, plain, a, b, c, f)
    have = range(HALO, HALO + RW)

    def slot(r):
        return r - HALO

    for i in (2, 3):
        put(acc, i, contribute(i, have, slot, w, m, a, b, f))
    middle_columns(acc, tall, act_in)
    for i in (0, 1, 4, 5):
        put(acc, i, contribute(i, have, slot, w, m, a, b, f))
    edge[...] = ring(range(6), have, slot, w, c)
    copy_k2.wait()
    middle(k2, mid, act_in)


def add_side(low, got, w, m, acc_in, edge_in, acc, edge, wide, plain, a, b, c, f):
    lay_out(lambda t: got[t].reshape(HALO * CL, C1), range(HALO), mean_matrix(C1), wide, plain, a, b, c, f)
    whole, part = 5 * low, 1 + 3 * low
    one = 2 * (1 - low)

    def lines(src, p, r):
        return src[p : p + FR, r].reshape(FR * 16, C2)

    blank = jnp.zeros((16, C2), BF)
    total = beside = None
    for p in range(3):
        left = jnp.concatenate(
            [
                jnp.concatenate([lines(src, p, r), blank if src is a else c[p, r]], axis=0)
                for r in range(HALO)
                for src in (a, b)
            ],
            axis=1,
        )
        one_left = jnp.concatenate(
            [jnp.concatenate([lines(src, p, one), blank if src is a else c[p, one]], axis=0) for src in (a, b)], axis=1
        )
        here = dot(left, w[p, pl.ds(low, HALO)].reshape(HALO * 512, C2))
        there = dot(one_left, w[p, 3 * low])
        total = here if total is None else total + here
        beside = there if beside is None else beside + there
    skip = jnp.concatenate([f[:, 1 - low + n].reshape(FR * 16, C2) for n in range(2)], axis=1)
    main = total[0 : FR * 16] + dot(skip, m[...])
    for i, sums, rim in ((whole, main, total), (part, beside[0 : FR * 16], beside)):
        for h in range(2):
            acc[h, :, i] = acc_in[h, :, i] + sums[:, h * 128 : (h + 1) * 128].reshape(FR, 16, 128)
        at = pl.ds(pl.multiple_of(i * 16, 16), 16)
        edge[at] = edge_in[at] + rim[FR * 16 : FR * 16 + 16]


def beside_far():
    return lax.axis_index("row") % FAR < 2


def near_kernel(got, w, m, acc_in, edge_in, acc, edge, *scratch):
    @pl.when(beside_far())
    def _():
        add_side(1 - lax.axis_index("row") % 2, got, w, m, acc_in, edge_in, acc, edge, *scratch)


def far_kernel(got, got_near, w, m, acc_in, edge_in, acc, edge, to_b, to_a, *scratch):
    low = lax.axis_index("row") % 2
    half = len(scratch) // 2

    def far():
        add_side(low, got, w, m, acc_in, edge_in, acc, edge, *scratch[:half])

    @pl.when(beside_far())
    def _():
        far()

    @pl.when(jnp.logical_not(beside_far()))
    def _():
        add_side(1 - low, got_near, w, m, acc_in, edge_in, acc, edge, *scratch[half:])
        far()

    odd = lax.axis_index("col") % 2 == 1
    flat = acc.reshape(2 * FR * 6 * 16, 128)

    def column(i, j):
        return jnp.concatenate(
            [flat[pl.ds(h * 768 + i * 16 + j, FR, stride=96), :] for h in range(2)], axis=1
        )

    for i in range(6):
        right = jnp.concatenate([column(i, 15), edge[i * 16 + 8 : i * 16 + 16]], axis=0)
        left = jnp.concatenate([edge[i * 16 : i * 16 + 8], column(i, 0)], axis=0)
        to_b[i] = jnp.where(odd, right, left).astype(BF)
        to_a[i] = jnp.where(odd, left, right).astype(BF)


OUTER = (0, 1, 4, 5)
FIXED = (0, 1, 14, 15)


def final_kernel(last_row, last_col, from_b, pair, acc, edge_in, k2, mid_in, out, mid, lv, edge, wide, a2, beside):
    row, col = lax.axis_index("row"), lax.axis_index("col")
    odd = col % 2 == 1
    for t in range(FR):
        for h in range(2):
            lv[h, t * 96 : (t + 1) * 96] = acc[h, t].reshape(96, 128)
    for i in range(6):
        fb = from_b[i].astype(F32)
        left = jnp.where(odd, pair[0, i].astype(F32), fb)
        right = jnp.where(odd, fb, pair[1, i].astype(F32))
        edge[i * 16 : i * 16 + 8] = edge_in[i * 16 : i * 16 + 8] + left[0:8]
        edge[i * 16 + 8 : i * 16 + 16] = edge_in[i * 16 + 8 : i * 16 + 16] + right[8:16]
        for h in range(2):
            half = slice(h * 128, (h + 1) * 128)
            lv[h, pl.ds(i * 16, FR, stride=96), :] += left[8:16, half]
            lv[h, pl.ds(i * 16 + 15, FR, stride=96), :] += right[0:8, half]

    def level(at, count):
        return jnp.concatenate([lv[0, at : at + count], lv[1, at : at + count]], axis=1)

    ones = mean_matrix(C2)
    keep = {i: jnp.float32(1.0) for i in range(6)}
    keep[0] = jnp.where(row == 0, 0.0, 1.0)
    keep[5] = jnp.where(row == last_row, 0.0, 1.0)
    keep_left = jnp.where(col == 0, 0.0, 1.0)
    keep_right = jnp.where(col == last_col, 0.0, 1.0)
    for t in range(FR):
        act = normed_silu(jnp.concatenate([level(t * 96, 32), level(t * 96 + 64, 32)], axis=0), ones)
        for k, i in enumerate(OUTER):
            base = (t * 4 + k) * 32 + 8
            kept = act[k * 16 : (k + 1) * 16] * keep[i]
            for h in range(2):
                wide[h, base : base + 16] = kept[:, h * 128 : (h + 1) * 128]

    def column(i, j):
        return jnp.concatenate([lv[h, pl.ds(i * 16 + j, FR, stride=96), :] for h in range(2)], axis=1)

    act = normed_silu(
        jnp.concatenate([edge[...]] + [column(i, j) for i in (2, 3) for j in (0, 15)], axis=0), ones
    )
    for k, i in enumerate(OUTER):
        for h in range(2):
            half = slice(h * 128, (h + 1) * 128)
            wide[h, pl.ds(k * 32 + 7, FR, stride=128), :] = act[i * 16 : i * 16 + 8, half] * (keep[i] * keep_left)
            wide[h, pl.ds(k * 32 + 24, FR, stride=128), :] = act[i * 16 + 8 : i * 16 + 16, half] * (
                keep[i] * keep_right
            )
    for n, i in enumerate((2, 3)):
        four = (
            act[i * 16 : i * 16 + 8] * keep_left,
            act[96 + n * 16 : 96 + n * 16 + 8],
            act[96 + n * 16 + 8 : 96 + n * 16 + 16],
            act[i * 16 + 8 : i * 16 + 16] * keep_right,
        )
        for v, value in enumerate(four):
            for h in range(2):
                beside[h, n, v, 0:8] = jnp.zeros((8, 128), F32)
                beside[h, n, v, 8:16] = value[:, h * 128 : (h + 1) * 128]
    for s in range(3):
        for k in range(4):
            for t in range(2):
                a2[s, t, k] = jnp.zeros((16, C2), BF)
            for t in range(FR):
                base = (t * 4 + k) * 32 + 7 + s
                for h in range(2):
                    a2[s, t + 2, k, :, h * 128 : (h + 1) * 128] = wide[h, base : base + 16].astype(BF)

    blank = jnp.zeros((FR, C2), F32)

    def fix(n, p, s):
        def at(v):
            return jnp.concatenate([beside[h, n, v, 6 + p : 14 + p] for h in range(2)], axis=1)

        rows = ((at(0), at(1), blank, blank), (at(1), blank, blank, at(2)), (blank, blank, at(2), at(3)))[s]
        return jnp.concatenate(rows, axis=0).astype(BF)

    for q in range(3):
        whole = [(i, OUTER.index(i + q)) for i in range(4) if i + q in OUTER]
        left = jnp.concatenate(
            [
                jnp.concatenate(
                    [a2[s, p : p + FR, k].reshape(FR * 16, C2) for _, k in whole] + [fix(n, p, s) for n in range(2)],
                    axis=0,
                )
                for p in range(3)
                for s in range(3)
            ],
            axis=1,
        )
        right = jnp.concatenate([k2[p, q].reshape(3 * C2, C2) for p in range(3)], axis=0)
        got = dot(left, right)
        for h in range(2):
            half = slice(h * 128, (h + 1) * 128)
            for n, (i, _) in enumerate(whole):
                mid[h, i * 128 : (i + 1) * 128] = (mid_in if q == 0 else mid)[h, i * 128 : (i + 1) * 128] + got[
                    n * 128 : (n + 1) * 128, half
                ]
            if q == 0:
                for i in range(4):
                    if i not in [i for i, _ in whole]:
                        mid[h, i * 128 : (i + 1) * 128] = mid_in[h, i * 128 : (i + 1) * 128]
            for n in range(2):
                for v, j in enumerate(FIXED):
                    at = pl.ds((2 - q + n) * 128 + j, FR, stride=16)
                    mid[h, at, :] += got[256 + n * 32 + v * 8 : 256 + n * 32 + v * 8 + 8, half]
    for t in range(FR):
        for i in range(4):
            at = (t * 6 + i + 1) * 16
            sums = jnp.concatenate([mid[h, i * 128 + t * 16 : i * 128 + t * 16 + 16] for h in range(2)], axis=1)
            out[t, i] = (level(at, 16) + sums).astype(BF)


def in_vmem(shape, dtype):
    return jax.ShapeDtypeStruct(shape, dtype)


def operands(rows):
    return [
        pltpu.VMEM(((FR + 2) * rows * PITCH, C1), F32),
        pltpu.VMEM((FR * rows * CL, C1), F32),
        pltpu.VMEM((FR + 2, rows, 16, C2), BF),
        pltpu.VMEM((FR + 2, rows, 16, C2), BF),
        pltpu.VMEM((3, rows, 16, C2), BF),
        pltpu.VMEM((FR, rows, 16, C2), BF),
    ]


ROWS_SHAPE = in_vmem((FR, HALO, CL, C1), BF)
W_SHAPE = in_vmem((3, 4, 512, C2), BF)
M_SHAPE = in_vmem((512, C2), BF)
ACC_SHAPE = in_vmem((2, FR, 6, 16, 128), F32)
MID_SHAPE = in_vmem((2, 4 * FR * 16, 128), F32)
EDGE_SHAPE = in_vmem((96, C2), F32)
STRIP_SHAPE = in_vmem((6, 16, C2), BF)
PARAMS = pltpu.CompilerParams(vmem_limit_bytes=24 * 2**20)


def in_hbm(x):
    return pltpu.with_memory_space_constraint(x, pltpu.HBM)


def first_part(feat, k1, proj):
    return pl.pallas_call(
        first_kernel,
        out_shape=(ROWS_SHAPE,) * 3 + (W_SHAPE, M_SHAPE) + tuple(in_vmem(x.shape, x.dtype) for x in (feat, k1)),
        in_specs=[HBM] * 3,
        out_specs=(VM,) * 7,
        scratch_shapes=[
            pltpu.SemaphoreType.DMA((2, FR)),
            pltpu.SemaphoreType.DMA,
            pltpu.VMEM(proj.shape, proj.dtype),
            pltpu.SemaphoreType.DMA((2,)),
        ],
        compiler_params=PARAMS,
        name="first_part",
    )(in_hbm(feat), in_hbm(k1), in_hbm(proj))


def own_part(feat, k1, proj, k2, w, m, feat_in, k1_in):
    return pl.pallas_call(
        own_kernel,
        out_shape=(W_SHAPE, M_SHAPE)
        + tuple(in_vmem(x.shape, x.dtype) for x in (feat, k1))
        + (ACC_SHAPE, EDGE_SHAPE, in_vmem(k2.shape, k2.dtype), MID_SHAPE),
        in_specs=[HBM] * 4 + [VM] * 4,
        out_specs=(VM,) * 8,
        scratch_shapes=[
            pltpu.VMEM(proj.shape, proj.dtype),
            pltpu.SemaphoreType.DMA((2,)),
            pltpu.SemaphoreType.DMA((2,)),
            pltpu.VMEM((2, FR * 2 * 32, 128), F32),
            pltpu.VMEM((3, FR + 2, 2, 16, C2), BF),
        ]
        + operands(RW),
        input_output_aliases={4: 0, 5: 1, 6: 2, 7: 3},
        compiler_params=PARAMS,
        name="own_part",
    )(in_hbm(feat), in_hbm(k1), in_hbm(proj), in_hbm(k2), w, m, feat_in, k1_in)


def near_part(got, w, m, acc, edge):
    return pl.pallas_call(
        near_kernel,
        out_shape=(ACC_SHAPE, EDGE_SHAPE),
        in_specs=[VM] * 5,
        out_specs=(VM,) * 2,
        scratch_shapes=operands(HALO),
        input_output_aliases={3: 0, 4: 1},
        compiler_params=PARAMS,
        name="near_part",
    )(got, w, m, acc, edge)


def far_part(got, got_near, w, m, acc, edge):
    return pl.pallas_call(
        far_kernel,
        out_shape=(ACC_SHAPE, EDGE_SHAPE, STRIP_SHAPE, STRIP_SHAPE),
        in_specs=[VM] * 6,
        out_specs=(VM,) * 4,
        scratch_shapes=operands(HALO) + operands(HALO),
        input_output_aliases={4: 0, 5: 1},
        compiler_params=PARAMS,
        name="far_part",
    )(got, got_near, w, m, acc, edge)


def final_part(last_row, last_col, from_b, pair, acc, edge, k2, mid):
    def kernel(*refs):
        final_kernel(last_row, last_col, *refs)

    return pl.pallas_call(
        kernel,
        out_shape=in_vmem((FR, 4, 16, C2), BF),
        in_specs=[VM] * 6,
        out_specs=VM,
        scratch_shapes=[
            pltpu.VMEM(MID_SHAPE.shape, F32),
            pltpu.VMEM((2, FR * 6 * 16, 128), F32),
            pltpu.VMEM((96, C2), F32),
            pltpu.VMEM((2, FR * 4 * 32, 128), F32),
            pltpu.VMEM((3, FR + 2, 4, 16, C2), BF),
            pltpu.VMEM((2, 2, 4, 16, 128), F32),
        ],
        compiler_params=PARAMS,
        name="final_part",
    )(from_b, pair, acc, edge, k2, mid)


def pairs(first, count):
    swaps = []
    for i in range(first, count - 1, 2):
        swaps += [(i, i + 1), (i + 1, i)]
    return swaps


def local(features, kernel_one, projection, kernel_two):
    rows, cols = lax.axis_size("row"), lax.axis_size("col")
    send_b, send_a, send_a_too, w, m, *here = first_part(features, kernel_one, projection)
    far_side = [(i, j) for i, j in pairs(0, rows) if min(i, j) % FAR == 0]
    others = [pair for pair in pairs(0, rows) if pair not in far_side]
    from_a = lax.ppermute(send_a, "row", far_side)
    from_b = lax.ppermute(send_b, "row", pairs(1, rows))
    from_a_too = lax.ppermute(send_a_too, "row", others)
    w, m, _, _, acc, edge, kernel_two, mid = own_part(features, kernel_one, projection, kernel_two, w, m, *here)
    acc, edge = near_part(from_a, w, m, acc, edge)
    acc, edge, to_b, to_a = far_part(from_b, from_a_too, w, m, acc, edge)
    from_b = lax.ppermute(to_b, "col", pairs(1, cols))
    pair = lax.all_gather(to_a, "col", axis_index_groups=[[i, i + 1] for i in range(0, cols, 2)])
    return final_part(rows - 1, cols - 1, from_b, pair, acc, edge, kernel_two, mid)


def solution(mesh):
    return jax.shard_map(
        local,
        mesh=mesh,
        in_specs=(P(None, "row", "col", None), P(), P(), P()),
        out_specs=P(None, "row", "col", None),
        check_vma=False,
    )
```

```python
import jax
import jax.numpy as jnp
from jax import lax
from jax.experimental import pallas as pl
from jax.experimental.pallas import tpu as pltpu
from jax.sharding import PartitionSpec as P

NORM_EPS = 1e-06
FR, RW, CL, C1, C2 = 8, 8, 32, 128, 256
HALO = 3
BF, F32 = jnp.bfloat16, jnp.float32
PITCH = 48
COLS_OF = (1, 2, 0, 3)
NEXT = 8
FAR = 16
VM = pl.BlockSpec(memory_space=pltpu.VMEM)
HBM = pl.BlockSpec(memory_space=pltpu.HBM)


def dot(a, b):
    return jnp.dot(a, b, preferred_element_type=F32)


def normed_silu(x, ones):
    mean = dot((x * x).astype(BF), ones)
    half = x * (0.5 * lax.rsqrt(mean + NORM_EPS))
    return half + half * jnp.tanh(half)


def mean_matrix(n):
    return jnp.full((n, n), 1.0 / n, BF)


def build_maps(proj, m):
    p0, p1, p2, p3 = (proj[i * C1 : (i + 1) * C1].astype(F32) * 0.5 for i in range(4))
    row = lax.broadcasted_iota(jnp.int32, (C1, C2), 0)
    col = lax.broadcasted_iota(jnp.int32, (C1, C2), 1)
    twice = jnp.where((col == row) | (col == row + C1), 0.5, 0.0).astype(F32)
    m[0:C1] = (p0 + p1 + p2 + p3 + twice).astype(BF)
    m[C1 : 2 * C1] = (p0 + p1 - p2 - p3 + twice).astype(BF)
    m[2 * C1 : 3 * C1] = (p0 - p1 + p2 - p3 + twice).astype(BF)
    m[3 * C1 : 4 * C1] = (p0 - p1 - p2 + p3 + twice).astype(BF)


def build_weights(frames, k1, w, m):
    zero = jnp.zeros((C1, C1), BF)

    def tap(p, q, s):
        return k1[p, q, s] if 0 <= s < 3 else zero

    for p in frames:
        for dr in range(4):
            pairs = [pr for pr in range(2) if 0 <= dr - pr < 3]
            left = jnp.concatenate(
                [
                    jnp.concatenate([tap(p, dr - pr, dc - pc) for pr in pairs for pc in range(2)], axis=1)
                    for dc in COLS_OF
                ],
                axis=0,
            )
            w[p, dr] = dot(left, m[pairs[0] * 256 : (pairs[-1] + 1) * 256]).astype(BF)


def lay_out(feature, row_of, ones, wide, plain, a, b, c, f):
    rows = len(row_of)
    span = rows * PITCH
    for t in range(2):
        for r, at in enumerate(row_of):
            base = t * span + r * PITCH
            wide[base + 8 : base + 16] = jnp.zeros((8, C1), F32)
            wide[base + 32 : base + 40] = jnp.zeros((8, C1), F32)
            a[t, at] = jnp.zeros((16, C2), BF)
            b[t, at] = jnp.zeros((16, C2), BF)
    for t in range(FR):
        x = feature(t).astype(F32)
        act = normed_silu(x, ones)
        for r, at in enumerate(row_of):
            base = (t + 2) * span + r * PITCH
            wide[base : base + 8] = jnp.zeros((8, C1), F32)
            wide[base + 40 : base + 48] = jnp.zeros((8, C1), F32)
            wide[base + 8 : base + 40] = act[r * CL : (r + 1) * CL]
            own = (t * rows + r) * CL
            plain[own : own + CL] = x[r * CL : (r + 1) * CL]
            a[t + 2, at, :, 0:C1] = wide[pl.ds(base + 8, 16, stride=2), :].astype(BF)
            a[t + 2, at, :, C1:C2] = wide[pl.ds(base + 9, 16, stride=2), :].astype(BF)
            b[t + 2, at, :, 0:C1] = wide[pl.ds(base + 7, 16, stride=2), :].astype(BF)
            b[t + 2, at, :, C1:C2] = wide[pl.ds(base + 10, 16, stride=2), :].astype(BF)
            f[t, at, :, 0:C1] = plain[pl.ds(own, 16, stride=2), :].astype(BF)
            f[t, at, :, C1:C2] = plain[pl.ds(own + 1, 16, stride=2), :].astype(BF)
    zero = jnp.zeros((FR, C1), F32)
    for p in range(3):
        for r, at in enumerate(row_of):
            base = p * span + r * PITCH + 8
            first = wide[pl.ds(base, FR, stride=span), :]
            last = wide[pl.ds(base + CL - 1, FR, stride=span), :]
            c[p, at, :, 0:C1] = jnp.concatenate([zero, last], axis=0).astype(BF)
            c[p, at, :, C1:C2] = jnp.concatenate([first, zero], axis=0).astype(BF)


def contribute(i, have, slot, w, m, a, b, f):
    total = None
    taps = [dr for dr in range(4) if 2 * i + dr in have]
    for p in range(3):
        left = jnp.concatenate(
            [src[p : p + FR, slot(2 * i + dr)].reshape(FR * 16, C2) for dr in taps for src in (a, b)], axis=1
        )
        right = w[p, taps[0] : taps[-1] + 1].reshape(len(taps) * 512, C2)
        got = dot(left, right)
        total = got if total is None else total + got
    for pr in range(2):
        if 2 * i + 1 + pr in have:
            total = total + dot(f[:, slot(2 * i + 1 + pr)].reshape(FR * 16, C2), m[pr * 256 : (pr + 1) * 256])
    return total


def ring(i_rows, have, slot, w, c):
    total = None
    blank = jnp.zeros((16, C2), BF)
    for dr in range(4):
        if not any(2 * i + dr in have for i in i_rows):
            continue
        for p in range(3):
            left = jnp.concatenate([c[p, slot(2 * i + dr)] if 2 * i + dr in have else blank for i in i_rows], axis=0)
            got = dot(left, w[p, dr, 256:512])
            total = got if total is None else total + got
    return total


def put(acc, i, got, old=None):
    for h in range(2):
        new = got[:, h * 128 : (h + 1) * 128].reshape(FR, 16, 128)
        acc[h, :, i] = new if old is None else old[h, :, i] + new


def early():
    return lax.axis_index("row") % FAR == 0


def waits():
    return lax.axis_index("row") % NEXT == 0


def first_kernel(
    feat, k1, proj, send_b, send_a, send_a_too, w, m, feat_in, k1_in, strip_sems, feat_sem, proj_in, sems
):
    last = (lax.axis_index("row") % 2) * (RW - HALO)

    def strips(n, begin, send):
        return [
            pltpu.make_async_copy(feat.at[t, pl.ds(begin, HALO)], send.at[t], strip_sems.at[n, t]) for t in range(FR)
        ]

    far = strips(0, last, send_b)
    for copy in far:
        copy.start()

    @pl.when(waits())
    def _():
        pltpu.make_async_copy(feat, feat_in, feat_sem).start()

    weights = [pltpu.make_async_copy(x, y, sems.at[n]) for n, (x, y) in enumerate([(k1, k1_in), (proj, proj_in)])]

    @pl.when(early())
    def _():
        for copy in weights:
            copy.start()

    for wanted, send in ((beside_far(), send_a), (jnp.logical_not(beside_far()), send_a_too)):

        @pl.when(wanted)
        def _(send=send):
            near = strips(1, RW - HALO - last, send)
            for copy in near:
                copy.start()
            for copy in near:
                copy.wait()

    for copy in far:
        copy.wait()

    @pl.when(waits())
    def _():
        pltpu.make_async_copy(feat, feat_in, feat_sem).wait()

    @pl.when(early())
    def _():
        for copy in weights:
            copy.wait()
        build_maps(proj_in, m)
        build_weights((0,), k1_in, w, m)


def middle_columns(acc, tall, act_in):
    x = jnp.concatenate([acc[h, :, 2:4].reshape(FR * 2 * 16, 128) for h in range(2)], axis=1)
    column = lax.broadcasted_iota(jnp.int32, (FR * 2 * 16, C2), 0) % 16
    inner = jnp.where((column > 0) & (column < 15), 1.0, 0.0).astype(F32)
    act = normed_silu(x, mean_matrix(C2)) * inner
    for n in range(2 * FR):
        for h in range(2):
            tall[h, n * 32 : n * 32 + 8] = jnp.zeros((8, 128), F32)
            tall[h, n * 32 + 24 : n * 32 + 32] = jnp.zeros((8, 128), F32)
            tall[h, n * 32 + 8 : n * 32 + 24] = act[n * 16 : (n + 1) * 16, h * 128 : (h + 1) * 128]
    for s in range(3):
        for n in range(2):
            for t in range(2):
                act_in[s, t, n] = jnp.zeros((16, C2), BF)
            for t in range(FR):
                base = (t * 2 + n) * 32 + 7 + s
                for h in range(2):
                    act_in[s, t + 2, n, :, h * 128 : (h + 1) * 128] = tall[h, base : base + 16].astype(BF)


def middle(k2, mid, act_in):
    for i in range(4):
        taps = [q for q in range(3) if i + q in (2, 3)]
        total = None
        for p in range(3):
            left = jnp.concatenate(
                [act_in[s, p : p + FR, i + q - 2].reshape(FR * 16, C2) for q in taps for s in range(3)], axis=1
            )
            got = dot(left, k2[p, taps[0] : taps[-1] + 1].reshape(len(taps) * 3 * C2, C2))
            total = got if total is None else total + got
        for h in range(2):
            mid[h, i * FR * 16 : (i + 1) * FR * 16] = total[:, h * 128 : (h + 1) * 128]


def own_kernel(
    feat, k1, proj, k2_far, w_in, m_in, feat_here, k1_here,
    w, m, feat_in, k1_in, acc, edge, k2, mid,
    proj_in, sems, late_sems, tall, act_in, wide, plain, a, b, c, f,
):
    copy = pltpu.make_async_copy(feat, feat_in, late_sems.at[0])

    @pl.when(jnp.logical_not(waits()))
    def _():
        copy.start()

    make = jnp.logical_not(early())
    sources = [
        pltpu.make_async_copy(x, y, sems.at[n]) for n, (x, y) in enumerate([(k1, k1_in), (proj, proj_in)])
    ]

    @pl.when(make)
    def _():
        for source in sources:
            source.start()

    @pl.when(jnp.logical_not(waits()))
    def _():
        copy.wait()

    @pl.when(make)
    def _():
        for source in sources:
            source.wait()

    copy_k2 = pltpu.make_async_copy(k2_far, k2, late_sems.at[1])
    copy_k2.start()

    @pl.when(make)
    def _():
        build_maps(proj_in, m)
        build_weights((0,), k1_in, w, m)

    build_weights((1, 2), k1_in, w, m)
    ones = mean_matrix(C1)
    lay_out(lambda t: feat_in[t].reshape(RW * CL, C1), range(RW), ones, wide, plain, a, b, c, f)
    have = range(HALO, HALO + RW)

    def slot(r):
        return r - HALO

    for i in (2, 3):
        put(acc, i, contribute(i, have, slot, w, m, a, b, f))
    middle_columns(acc, tall, act_in)
    for i in (0, 1, 4, 5):
        put(acc, i, contribute(i, have, slot, w, m, a, b, f))
    edge[...] = ring(range(6), have, slot, w, c)
    copy_k2.wait()
    middle(k2, mid, act_in)


def add_side(low, got, w, m, acc_in, edge_in, acc, edge, wide, plain, a, b, c, f):
    lay_out(lambda t: got[t].reshape(HALO * CL, C1), range(HALO), mean_matrix(C1), wide, plain, a, b, c, f)
    whole, part = 5 * low, 1 + 3 * low
    one = 2 * (1 - low)

    def lines(src, p, r):
        return src[p : p + FR, r].reshape(FR * 16, C2)

    blank = jnp.zeros((16, C2), BF)
    total = beside = None
    for p in range(3):
        left = jnp.concatenate(
            [
                jnp.concatenate([lines(src, p, r), blank if src is a else c[p, r]], axis=0)
                for r in range(HALO)
                for src in (a, b)
            ],
            axis=1,
        )
        one_left = jnp.concatenate(
            [jnp.concatenate([lines(src, p, one), blank if src is a else c[p, one]], axis=0) for src in (a, b)], axis=1
        )
        here = dot(left, w[p, pl.ds(low, HALO)].reshape(HALO * 512, C2))
        there = dot(one_left, w[p, 3 * low])
        total = here if total is None else total + here
        beside = there if beside is None else beside + there
    skip = jnp.concatenate([f[:, 1 - low + n].reshape(FR * 16, C2) for n in range(2)], axis=1)
    main = total[0 : FR * 16] + dot(skip, m[...])
    for i, sums, rim in ((whole, main, total), (part, beside[0 : FR * 16], beside)):
        for h in range(2):
            acc[h, :, i] = acc_in[h, :, i] + sums[:, h * 128 : (h + 1) * 128].reshape(FR, 16, 128)
        at = pl.ds(pl.multiple_of(i * 16, 16), 16)
        edge[at] = edge_in[at] + rim[FR * 16 : FR * 16 + 16]


def beside_far():
    return lax.axis_index("row") % FAR < 2


def near_kernel(got, w, m, acc_in, edge_in, acc, edge, *scratch):
    @pl.when(beside_far())
    def _():
        add_side(1 - lax.axis_index("row") % 2, got, w, m, acc_in, edge_in, acc, edge, *scratch)


def far_kernel(got, got_near, w, m, acc_in, edge_in, acc, edge, to_b, to_a, *scratch):
    low = lax.axis_index("row") % 2
    half = len(scratch) // 2

    def far():
        add_side(low, got, w, m, acc_in, edge_in, acc, edge, *scratch[:half])

    @pl.when(beside_far())
    def _():
        far()

    @pl.when(jnp.logical_not(beside_far()))
    def _():
        add_side(1 - low, got_near, w, m, acc_in, edge_in, acc, edge, *scratch[half:])
        far()

    odd = lax.axis_index("col") % 2 == 1
    flat = acc.reshape(2 * FR * 6 * 16, 128)

    def column(i, j):
        return jnp.concatenate(
            [flat[pl.ds(h * 768 + i * 16 + j, FR, stride=96), :] for h in range(2)], axis=1
        )

    for i in range(6):
        right = jnp.concatenate([column(i, 15), edge[i * 16 + 8 : i * 16 + 16]], axis=0)
        left = jnp.concatenate([edge[i * 16 : i * 16 + 8], column(i, 0)], axis=0)
        to_b[i] = jnp.where(odd, right, left).astype(BF)
        to_a[i] = jnp.where(odd, left, right).astype(BF)


OUTER = (0, 1, 4, 5)
FIXED = (0, 1, 14, 15)


def final_kernel(
    last_row, last_col, from_b, pair, acc_in, edge_in, k2, mid_in, out, acc, mid, edge, wide, a2, beside
):
    row, col = lax.axis_index("row"), lax.axis_index("col")
    odd = col % 2 == 1
    flat = acc.reshape(2 * FR * 6 * 16, 128)

    def lines(h, i, j):
        return pl.ds(h * FR * 96 + i * 16 + j, FR, stride=96)

    for i in range(6):
        fb = from_b[i].astype(F32)
        left = jnp.where(odd, pair[0, i].astype(F32), fb)
        right = jnp.where(odd, fb, pair[1, i].astype(F32))
        edge[i * 16 : i * 16 + 8] = edge_in[i * 16 : i * 16 + 8] + left[0:8]
        edge[i * 16 + 8 : i * 16 + 16] = edge_in[i * 16 + 8 : i * 16 + 16] + right[8:16]
        for h in range(2):
            half = slice(h * 128, (h + 1) * 128)
            flat[lines(h, i, 0), :] += left[8:16, half]
            flat[lines(h, i, 15), :] += right[0:8, half]

    ones = mean_matrix(C2)
    keep = {i: jnp.float32(1.0) for i in range(6)}
    keep[0] = jnp.where(row == 0, 0.0, 1.0)
    keep[5] = jnp.where(row == last_row, 0.0, 1.0)
    keep_left = jnp.where(col == 0, 0.0, 1.0)
    keep_right = jnp.where(col == last_col, 0.0, 1.0)

    def column(i, j):
        return jnp.concatenate([flat[lines(h, i, j), :] for h in range(2)], axis=1)

    rim = normed_silu(
        jnp.concatenate([edge[...]] + [column(i, j) for i in (2, 3) for j in (0, 15)], axis=0), ones
    )
    for n, i in enumerate((2, 3)):
        four = (
            rim[i * 16 : i * 16 + 8] * keep_left,
            rim[96 + n * 16 : 96 + n * 16 + 8],
            rim[96 + n * 16 + 8 : 96 + n * 16 + 16],
            rim[i * 16 + 8 : i * 16 + 16] * keep_right,
        )
        for v, value in enumerate(four):
            for h in range(2):
                beside[h, n, v, 0:8] = jnp.zeros((8, 128), F32)
                beside[h, n, v, 8:16] = value[:, h * 128 : (h + 1) * 128]

    def activate(k):
        i = OUTER[k]
        x = jnp.concatenate([acc[h, :, i].reshape(FR * 16, 128) for h in range(2)], axis=1)
        act = normed_silu(x, ones) * keep[i]
        for h in range(2):
            half = slice(h * 128, (h + 1) * 128)
            for t in range(FR):
                base = (t * 4 + k) * 32 + 8
                wide[h, base : base + 16] = act[t * 16 : (t + 1) * 16, half]
            wide[h, pl.ds(k * 32 + 7, FR, stride=128), :] = rim[i * 16 : i * 16 + 8, half] * (keep[i] * keep_left)
            wide[h, pl.ds(k * 32 + 24, FR, stride=128), :] = rim[i * 16 + 8 : i * 16 + 16, half] * (
                keep[i] * keep_right
            )
        for s in range(3):
            for t in range(2):
                a2[s, t, k] = jnp.zeros((16, C2), BF)
            for t in range(FR):
                base = (t * 4 + k) * 32 + 7 + s
                for h in range(2):
                    a2[s, t + 2, k, :, h * 128 : (h + 1) * 128] = wide[h, base : base + 16].astype(BF)

    blank = jnp.zeros((FR, C2), F32)

    def fix(n, p, s):
        def at(v):
            return jnp.concatenate([beside[h, n, v, 6 + p : 14 + p] for h in range(2)], axis=1)

        rows = ((at(0), at(1), blank, blank), (at(1), blank, blank, at(2)), (blank, blank, at(2), at(3)))[s]
        return jnp.concatenate(rows, axis=0).astype(BF)

    def convolve(q):
        whole = [(i, OUTER.index(i + q)) for i in range(4) if i + q in OUTER]
        left = jnp.concatenate(
            [
                jnp.concatenate(
                    [a2[s, p : p + FR, k].reshape(FR * 16, C2) for _, k in whole] + [fix(n, p, s) for n in range(2)],
                    axis=0,
                )
                for p in range(3)
                for s in range(3)
            ],
            axis=1,
        )
        right = jnp.concatenate([k2[p, q].reshape(3 * C2, C2) for p in range(3)], axis=0)
        got = dot(left, right)
        for h in range(2):
            half = slice(h * 128, (h + 1) * 128)
            for n, (i, _) in enumerate(whole):
                mid[h, i * 128 : (i + 1) * 128] += got[n * 128 : (n + 1) * 128, half]
            for n in range(2):
                for v, j in enumerate(FIXED):
                    at = pl.ds((2 - q + n) * 128 + j, FR, stride=16)
                    mid[h, at, :] += got[256 + n * 32 + v * 8 : 256 + n * 32 + v * 8 + 8, half]

    activate(0)
    activate(1)
    convolve(0)
    activate(2)
    activate(3)
    convolve(2)
    convolve(1)
    for t in range(FR):
        for i in range(4):
            sums = jnp.concatenate(
                [acc[h, t, i + 1] + mid[h, i * 128 + t * 16 : i * 128 + t * 16 + 16] for h in range(2)], axis=1
            )
            out[t, i] = sums.astype(BF)


def in_vmem(shape, dtype):
    return jax.ShapeDtypeStruct(shape, dtype)


def operands(rows):
    return [
        pltpu.VMEM(((FR + 2) * rows * PITCH, C1), F32),
        pltpu.VMEM((FR * rows * CL, C1), F32),
        pltpu.VMEM((FR + 2, rows, 16, C2), BF),
        pltpu.VMEM((FR + 2, rows, 16, C2), BF),
        pltpu.VMEM((3, rows, 16, C2), BF),
        pltpu.VMEM((FR, rows, 16, C2), BF),
    ]


ROWS_SHAPE = in_vmem((FR, HALO, CL, C1), BF)
W_SHAPE = in_vmem((3, 4, 512, C2), BF)
M_SHAPE = in_vmem((512, C2), BF)
ACC_SHAPE = in_vmem((2, FR, 6, 16, 128), F32)
MID_SHAPE = in_vmem((2, 4 * FR * 16, 128), F32)
EDGE_SHAPE = in_vmem((96, C2), F32)
STRIP_SHAPE = in_vmem((6, 16, C2), BF)
PARAMS = pltpu.CompilerParams(vmem_limit_bytes=24 * 2**20)


def in_hbm(x):
    return pltpu.with_memory_space_constraint(x, pltpu.HBM)


def held(*xs):
    return tuple(pltpu.with_memory_space_constraint(x, pltpu.VMEM) for x in xs)


def first_part(feat, k1, proj):
    return pl.pallas_call(
        first_kernel,
        out_shape=(ROWS_SHAPE,) * 3 + (W_SHAPE, M_SHAPE) + tuple(in_vmem(x.shape, x.dtype) for x in (feat, k1)),
        in_specs=[HBM] * 3,
        out_specs=(VM,) * 7,
        scratch_shapes=[
            pltpu.SemaphoreType.DMA((2, FR)),
            pltpu.SemaphoreType.DMA,
            pltpu.VMEM(proj.shape, proj.dtype),
            pltpu.SemaphoreType.DMA((2,)),
        ],
        compiler_params=PARAMS,
        name="first_part",
    )(in_hbm(feat), in_hbm(k1), in_hbm(proj))


def own_part(feat, k1, proj, k2, w, m, feat_in, k1_in):
    return pl.pallas_call(
        own_kernel,
        out_shape=(W_SHAPE, M_SHAPE)
        + tuple(in_vmem(x.shape, x.dtype) for x in (feat, k1))
        + (ACC_SHAPE, EDGE_SHAPE, in_vmem(k2.shape, k2.dtype), MID_SHAPE),
        in_specs=[HBM] * 4 + [VM] * 4,
        out_specs=(VM,) * 8,
        scratch_shapes=[
            pltpu.VMEM(proj.shape, proj.dtype),
            pltpu.SemaphoreType.DMA((2,)),
            pltpu.SemaphoreType.DMA((2,)),
            pltpu.VMEM((2, FR * 2 * 32, 128), F32),
            pltpu.VMEM((3, FR + 2, 2, 16, C2), BF),
        ]
        + operands(RW),
        input_output_aliases={4: 0, 5: 1, 6: 2, 7: 3},
        compiler_params=PARAMS,
        name="own_part",
    )(in_hbm(feat), in_hbm(k1), in_hbm(proj), in_hbm(k2), *held(w, m, feat_in, k1_in))


def near_part(got, w, m, acc, edge):
    return pl.pallas_call(
        near_kernel,
        out_shape=(ACC_SHAPE, EDGE_SHAPE),
        in_specs=[VM] * 5,
        out_specs=(VM,) * 2,
        scratch_shapes=operands(HALO),
        input_output_aliases={3: 0, 4: 1},
        compiler_params=PARAMS,
        name="near_part",
    )(got, w, m, *held(acc, edge))


def far_part(got, got_near, w, m, acc, edge):
    return pl.pallas_call(
        far_kernel,
        out_shape=(ACC_SHAPE, EDGE_SHAPE, STRIP_SHAPE, STRIP_SHAPE),
        in_specs=[VM] * 6,
        out_specs=(VM,) * 4,
        scratch_shapes=operands(HALO) + operands(HALO),
        input_output_aliases={4: 0, 5: 1},
        compiler_params=PARAMS,
        name="far_part",
    )(got, got_near, w, m, *held(acc, edge))


def final_part(last_row, last_col, from_b, pair, acc, edge, k2, mid):
    def kernel(*refs):
        final_kernel(last_row, last_col, *refs)

    return pl.pallas_call(
        kernel,
        out_shape=(in_vmem((FR, 4, 16, C2), BF), ACC_SHAPE, MID_SHAPE),
        in_specs=[VM] * 6,
        out_specs=(VM,) * 3,
        scratch_shapes=[
            pltpu.VMEM((96, C2), F32),
            pltpu.VMEM((2, FR * 4 * 32, 128), F32),
            pltpu.VMEM((3, FR + 2, 4, 16, C2), BF),
            pltpu.VMEM((2, 2, 4, 16, 128), F32),
        ],
        input_output_aliases={2: 1, 5: 2},
        compiler_params=PARAMS,
        name="final_part",
    )(from_b, pair, *held(acc), edge, k2, *held(mid))[0]


def pairs(first, count):
    swaps = []
    for i in range(first, count - 1, 2):
        swaps += [(i, i + 1), (i + 1, i)]
    return swaps


def local(features, kernel_one, projection, kernel_two):
    rows, cols = lax.axis_size("row"), lax.axis_size("col")
    send_b, send_a, send_a_too, w, m, *here = first_part(features, kernel_one, projection)
    far_side = [(i, j) for i, j in pairs(0, rows) if min(i, j) % FAR == 0]
    others = [pair for pair in pairs(0, rows) if pair not in far_side]
    from_a = lax.ppermute(send_a, "row", far_side)
    from_b = lax.ppermute(send_b, "row", pairs(1, rows))
    from_a_too = lax.ppermute(send_a_too, "row", others)
    w, m, _, _, acc, edge, kernel_two, mid = own_part(features, kernel_one, projection, kernel_two, w, m, *here)
    acc, edge = near_part(from_a, w, m, acc, edge)
    acc, edge, to_b, to_a = far_part(from_b, from_a_too, w, m, acc, edge)
    from_b = lax.ppermute(to_b, "col", pairs(1, cols))
    pair = lax.all_gather(to_a, "col", axis_index_groups=[[i, i + 1] for i in range(0, cols, 2)])
    return final_part(rows - 1, cols - 1, from_b, pair, acc, edge, kernel_two, mid)


def solution(mesh):
    return jax.shard_map(
        local,
        mesh=mesh,
        in_specs=(P(None, "row", "col", None), P(), P(), P()),
        out_specs=P(None, "row", "col", None),
        check_vma=False,
    )
```

```python
import jax
import jax.numpy as jnp
from jax import lax
from jax.experimental import pallas as pl
from jax.experimental.pallas import tpu as pltpu
from jax.sharding import PartitionSpec as P

NORM_EPS = 1e-06
FR, RW, CL, C1, C2 = 8, 8, 32, 128, 256
HALO = 3
BF, F32 = jnp.bfloat16, jnp.float32
PITCH = 48
COLS_OF = (1, 2, 0, 3)
NEXT = 8
FAR = 16
VM = pl.BlockSpec(memory_space=pltpu.VMEM)
HBM = pl.BlockSpec(memory_space=pltpu.HBM)


def dot(a, b):
    return jnp.dot(a, b, preferred_element_type=F32)


def normed_silu(x, ones):
    mean = dot((x * x).astype(BF), ones)
    half = x * (0.5 * lax.rsqrt(mean + NORM_EPS))
    return half + half * jnp.tanh(half)


def mean_matrix(n):
    return jnp.full((n, n), 1.0 / n, BF)


def build_maps(proj, m):
    p0, p1, p2, p3 = (proj[i * C1 : (i + 1) * C1].astype(F32) * 0.5 for i in range(4))
    row = lax.broadcasted_iota(jnp.int32, (C1, C2), 0)
    col = lax.broadcasted_iota(jnp.int32, (C1, C2), 1)
    twice = jnp.where((col == row) | (col == row + C1), 0.5, 0.0).astype(F32)
    m[0:C1] = (p0 + p1 + p2 + p3 + twice).astype(BF)
    m[C1 : 2 * C1] = (p0 + p1 - p2 - p3 + twice).astype(BF)
    m[2 * C1 : 3 * C1] = (p0 - p1 + p2 - p3 + twice).astype(BF)
    m[3 * C1 : 4 * C1] = (p0 - p1 - p2 + p3 + twice).astype(BF)


def build_weights(frames, k1, w, m):
    zero = jnp.zeros((C1, C1), BF)

    def tap(p, q, s):
        return k1[p, q, s] if 0 <= s < 3 else zero

    for p in frames:
        for dr in range(4):
            pairs = [pr for pr in range(2) if 0 <= dr - pr < 3]
            left = jnp.concatenate(
                [
                    jnp.concatenate([tap(p, dr - pr, dc - pc) for pr in pairs for pc in range(2)], axis=1)
                    for dc in COLS_OF
                ],
                axis=0,
            )
            w[p, dr] = dot(left, m[pairs[0] * 256 : (pairs[-1] + 1) * 256]).astype(BF)


def lay_out(feature, row_of, ones, wide, plain, a, b, c, f):
    rows = len(row_of)
    span = rows * PITCH
    for t in range(2):
        for r, at in enumerate(row_of):
            base = t * span + r * PITCH
            wide[base + 8 : base + 16] = jnp.zeros((8, C1), F32)
            wide[base + 32 : base + 40] = jnp.zeros((8, C1), F32)
            a[t, at] = jnp.zeros((16, C2), BF)
            b[t, at] = jnp.zeros((16, C2), BF)
    for t in range(FR):
        x = feature(t).astype(F32)
        act = normed_silu(x, ones)
        for r, at in enumerate(row_of):
            base = (t + 2) * span + r * PITCH
            wide[base : base + 8] = jnp.zeros((8, C1), F32)
            wide[base + 40 : base + 48] = jnp.zeros((8, C1), F32)
            wide[base + 8 : base + 40] = act[r * CL : (r + 1) * CL]
            own = (t * rows + r) * CL
            plain[own : own + CL] = x[r * CL : (r + 1) * CL]
            a[t + 2, at, :, 0:C1] = wide[pl.ds(base + 8, 16, stride=2), :].astype(BF)
            a[t + 2, at, :, C1:C2] = wide[pl.ds(base + 9, 16, stride=2), :].astype(BF)
            b[t + 2, at, :, 0:C1] = wide[pl.ds(base + 7, 16, stride=2), :].astype(BF)
            b[t + 2, at, :, C1:C2] = wide[pl.ds(base + 10, 16, stride=2), :].astype(BF)
            f[t, at, :, 0:C1] = plain[pl.ds(own, 16, stride=2), :].astype(BF)
            f[t, at, :, C1:C2] = plain[pl.ds(own + 1, 16, stride=2), :].astype(BF)
    zero = jnp.zeros((FR, C1), F32)
    for p in range(3):
        for r, at in enumerate(row_of):
            base = p * span + r * PITCH + 8
            first = wide[pl.ds(base, FR, stride=span), :]
            last = wide[pl.ds(base + CL - 1, FR, stride=span), :]
            c[p, at, :, 0:C1] = jnp.concatenate([zero, last], axis=0).astype(BF)
            c[p, at, :, C1:C2] = jnp.concatenate([first, zero], axis=0).astype(BF)


def contribute(i, have, slot, w, m, a, b, f):
    total = None
    taps = [dr for dr in range(4) if 2 * i + dr in have]
    for p in range(3):
        left = jnp.concatenate(
            [src[p : p + FR, slot(2 * i + dr)].reshape(FR * 16, C2) for dr in taps for src in (a, b)], axis=1
        )
        right = w[p, taps[0] : taps[-1] + 1].reshape(len(taps) * 512, C2)
        got = dot(left, right)
        total = got if total is None else total + got
    for pr in range(2):
        if 2 * i + 1 + pr in have:
            total = total + dot(f[:, slot(2 * i + 1 + pr)].reshape(FR * 16, C2), m[pr * 256 : (pr + 1) * 256])
    return total


def ring(i_rows, have, slot, w, c):
    total = None
    blank = jnp.zeros((16, C2), BF)
    for dr in range(4):
        if not any(2 * i + dr in have for i in i_rows):
            continue
        for p in range(3):
            left = jnp.concatenate([c[p, slot(2 * i + dr)] if 2 * i + dr in have else blank for i in i_rows], axis=0)
            got = dot(left, w[p, dr, 256:512])
            total = got if total is None else total + got
    return total


def put(acc, i, got, old=None):
    for h in range(2):
        new = got[:, h * 128 : (h + 1) * 128].reshape(FR, 16, 128)
        acc[h, :, i] = new if old is None else old[h, :, i] + new


def early():
    return lax.axis_index("row") % FAR == 0


def waits():
    return lax.axis_index("row") % NEXT == 0


def first_kernel(
    feat, k1, proj, send_b, send_a, send_a_too, w, m, feat_in, k1_in, strip_sems, feat_sem, proj_in, sems
):
    last = (lax.axis_index("row") % 2) * (RW - HALO)

    def strips(n, begin, send):
        return [
            pltpu.make_async_copy(feat.at[t, pl.ds(begin, HALO)], send.at[t], strip_sems.at[n, t]) for t in range(FR)
        ]

    far = strips(0, last, send_b)
    for copy in far:
        copy.start()

    @pl.when(waits())
    def _():
        pltpu.make_async_copy(feat, feat_in, feat_sem).start()

    weights = [pltpu.make_async_copy(x, y, sems.at[n]) for n, (x, y) in enumerate([(k1, k1_in), (proj, proj_in)])]

    @pl.when(early())
    def _():
        for copy in weights:
            copy.start()

    for wanted, send in ((beside_far(), send_a), (jnp.logical_not(beside_far()), send_a_too)):

        @pl.when(wanted)
        def _(send=send):
            near = strips(1, RW - HALO - last, send)
            for copy in near:
                copy.start()
            for copy in near:
                copy.wait()

    for copy in far:
        copy.wait()

    @pl.when(waits())
    def _():
        pltpu.make_async_copy(feat, feat_in, feat_sem).wait()

    @pl.when(early())
    def _():
        for copy in weights:
            copy.wait()
        build_maps(proj_in, m)
        build_weights((0, 1), k1_in, w, m)


def middle_columns(acc, tall, act_in):
    x = jnp.concatenate([acc[h, :, 2:4].reshape(FR * 2 * 16, 128) for h in range(2)], axis=1)
    column = lax.broadcasted_iota(jnp.int32, (FR * 2 * 16, C2), 0) % 16
    inner = jnp.where((column > 0) & (column < 15), 1.0, 0.0).astype(F32)
    act = normed_silu(x, mean_matrix(C2)) * inner
    for n in range(2 * FR):
        for h in range(2):
            tall[h, n * 32 : n * 32 + 8] = jnp.zeros((8, 128), F32)
            tall[h, n * 32 + 24 : n * 32 + 32] = jnp.zeros((8, 128), F32)
            tall[h, n * 32 + 8 : n * 32 + 24] = act[n * 16 : (n + 1) * 16, h * 128 : (h + 1) * 128]
    for s in range(3):
        for n in range(2):
            for t in range(2):
                act_in[s, t, n] = jnp.zeros((16, C2), BF)
            for t in range(FR):
                base = (t * 2 + n) * 32 + 7 + s
                for h in range(2):
                    act_in[s, t + 2, n, :, h * 128 : (h + 1) * 128] = tall[h, base : base + 16].astype(BF)


def middle(k2, mid, act_in):
    for i in range(4):
        taps = [q for q in range(3) if i + q in (2, 3)]
        total = None
        for p in range(3):
            left = jnp.concatenate(
                [act_in[s, p : p + FR, i + q - 2].reshape(FR * 16, C2) for q in taps for s in range(3)], axis=1
            )
            got = dot(left, k2[p, taps[0] : taps[-1] + 1].reshape(len(taps) * 3 * C2, C2))
            total = got if total is None else total + got
        for h in range(2):
            mid[h, i * FR * 16 : (i + 1) * FR * 16] = total[:, h * 128 : (h + 1) * 128]


def own_kernel(
    feat, k1, proj, k2_far, w_in, m_in, feat_here, k1_here,
    w, m, feat_in, k1_in, acc, edge, k2, mid,
    proj_in, sems, late_sems, tall, act_in, wide, plain, a, b, c, f,
):
    copy = pltpu.make_async_copy(feat, feat_in, late_sems.at[0])

    @pl.when(jnp.logical_not(waits()))
    def _():
        copy.start()

    make = jnp.logical_not(early())
    sources = [
        pltpu.make_async_copy(x, y, sems.at[n]) for n, (x, y) in enumerate([(k1, k1_in), (proj, proj_in)])
    ]

    @pl.when(make)
    def _():
        for source in sources:
            source.start()

    @pl.when(jnp.logical_not(waits()))
    def _():
        copy.wait()

    copy_k2 = pltpu.make_async_copy(k2_far, k2, late_sems.at[1])

    def rest(frames):
        copy_k2.start()
        build_weights(frames, k1_in, w, m)
        ones = mean_matrix(C1)
        lay_out(lambda t: feat_in[t].reshape(RW * CL, C1), range(RW), ones, wide, plain, a, b, c, f)
        have = range(HALO, HALO + RW)

        def slot(r):
            return r - HALO

        for i in (2, 3):
            put(acc, i, contribute(i, have, slot, w, m, a, b, f))
        middle_columns(acc, tall, act_in)
        for i in (0, 1, 4, 5):
            put(acc, i, contribute(i, have, slot, w, m, a, b, f))
        edge[...] = ring(range(6), have, slot, w, c)
        copy_k2.wait()
        middle(k2, mid, act_in)

    @pl.when(make)
    def _():
        for source in sources:
            source.wait()
        build_maps(proj_in, m)
        rest((0, 1, 2))

    @pl.when(early())
    def _():
        rest((2,))


def add_side(low, got, w, m, acc_in, edge_in, acc, edge, wide, plain, a, b, c, f):
    lay_out(lambda t: got[t].reshape(HALO * CL, C1), range(HALO), mean_matrix(C1), wide, plain, a, b, c, f)
    whole, part = 5 * low, 1 + 3 * low
    one = 2 * (1 - low)

    def lines(src, p, r):
        return src[p : p + FR, r].reshape(FR * 16, C2)

    blank = jnp.zeros((16, C2), BF)
    total = beside = None
    for p in range(3):
        left = jnp.concatenate(
            [
                jnp.concatenate([lines(src, p, r), blank if src is a else c[p, r]], axis=0)
                for r in range(HALO)
                for src in (a, b)
            ],
            axis=1,
        )
        one_left = jnp.concatenate(
            [jnp.concatenate([lines(src, p, one), blank if src is a else c[p, one]], axis=0) for src in (a, b)], axis=1
        )
        here = dot(left, w[p, pl.ds(low, HALO)].reshape(HALO * 512, C2))
        there = dot(one_left, w[p, 3 * low])
        total = here if total is None else total + here
        beside = there if beside is None else beside + there
    skip = jnp.concatenate([f[:, 1 - low + n].reshape(FR * 16, C2) for n in range(2)], axis=1)
    main = total[0 : FR * 16] + dot(skip, m[...])
    for i, sums, rim in ((whole, main, total), (part, beside[0 : FR * 16], beside)):
        for h in range(2):
            acc[h, :, i] = acc_in[h, :, i] + sums[:, h * 128 : (h + 1) * 128].reshape(FR, 16, 128)
        at = pl.ds(pl.multiple_of(i * 16, 16), 16)
        edge[at] = edge_in[at] + rim[FR * 16 : FR * 16 + 16]


def beside_far():
    return lax.axis_index("row") % FAR < 2


def near_kernel(got, w, m, acc_in, edge_in, acc, edge, *scratch):
    @pl.when(beside_far())
    def _():
        add_side(1 - lax.axis_index("row") % 2, got, w, m, acc_in, edge_in, acc, edge, *scratch)


def far_kernel(got, got_near, w, m, acc_in, edge_in, acc, edge, to_b, to_a, *scratch):
    low = lax.axis_index("row") % 2
    half = len(scratch) // 2

    def far():
        add_side(low, got, w, m, acc_in, edge_in, acc, edge, *scratch[:half])

    @pl.when(beside_far())
    def _():
        far()

    @pl.when(jnp.logical_not(beside_far()))
    def _():
        add_side(1 - low, got_near, w, m, acc_in, edge_in, acc, edge, *scratch[half:])
        far()

    odd = lax.axis_index("col") % 2 == 1
    flat = acc.reshape(2 * FR * 6 * 16, 128)

    def column(i, j):
        return jnp.concatenate(
            [flat[pl.ds(h * 768 + i * 16 + j, FR, stride=96), :] for h in range(2)], axis=1
        )

    for i in range(6):
        right = jnp.concatenate([column(i, 15), edge[i * 16 + 8 : i * 16 + 16]], axis=0)
        left = jnp.concatenate([edge[i * 16 : i * 16 + 8], column(i, 0)], axis=0)
        to_b[i] = jnp.where(odd, right, left).astype(BF)
        to_a[i] = jnp.where(odd, left, right).astype(BF)


OUTER = (0, 1, 4, 5)
FIXED = (0, 1, 14, 15)


def final_kernel(
    last_row, last_col, from_b, pair, acc_in, edge_in, k2, mid_in, out, acc, mid, edge, wide, a2, beside
):
    row, col = lax.axis_index("row"), lax.axis_index("col")
    odd = col % 2 == 1
    flat = acc.reshape(2 * FR * 6 * 16, 128)

    def lines(h, i, j):
        return pl.ds(h * FR * 96 + i * 16 + j, FR, stride=96)

    for i in range(6):
        fb = from_b[i].astype(F32)
        left = jnp.where(odd, pair[0, i].astype(F32), fb)
        right = jnp.where(odd, fb, pair[1, i].astype(F32))
        edge[i * 16 : i * 16 + 8] = edge_in[i * 16 : i * 16 + 8] + left[0:8]
        edge[i * 16 + 8 : i * 16 + 16] = edge_in[i * 16 + 8 : i * 16 + 16] + right[8:16]
        for h in range(2):
            half = slice(h * 128, (h + 1) * 128)
            flat[lines(h, i, 0), :] += left[8:16, half]
            flat[lines(h, i, 15), :] += right[0:8, half]

    ones = mean_matrix(C2)
    keep = {i: jnp.float32(1.0) for i in range(6)}
    keep[0] = jnp.where(row == 0, 0.0, 1.0)
    keep[5] = jnp.where(row == last_row, 0.0, 1.0)
    keep_left = jnp.where(col == 0, 0.0, 1.0)
    keep_right = jnp.where(col == last_col, 0.0, 1.0)

    def column(i, j):
        return jnp.concatenate([flat[lines(h, i, j), :] for h in range(2)], axis=1)

    rim = normed_silu(
        jnp.concatenate([edge[...]] + [column(i, j) for i in (2, 3) for j in (0, 15)], axis=0), ones
    )
    for n, i in enumerate((2, 3)):
        four = (
            rim[i * 16 : i * 16 + 8] * keep_left,
            rim[96 + n * 16 : 96 + n * 16 + 8],
            rim[96 + n * 16 + 8 : 96 + n * 16 + 16],
            rim[i * 16 + 8 : i * 16 + 16] * keep_right,
        )
        for v, value in enumerate(four):
            for h in range(2):
                beside[h, n, v, 0:8] = jnp.zeros((8, 128), F32)
                beside[h, n, v, 8:16] = value[:, h * 128 : (h + 1) * 128]

    def activate(k):
        i = OUTER[k]
        x = jnp.concatenate([acc[h, :, i].reshape(FR * 16, 128) for h in range(2)], axis=1)
        act = normed_silu(x, ones) * keep[i]
        for h in range(2):
            half = slice(h * 128, (h + 1) * 128)
            for t in range(FR):
                base = (t * 4 + k) * 32 + 8
                wide[h, base : base + 16] = act[t * 16 : (t + 1) * 16, half]
            wide[h, pl.ds(k * 32 + 7, FR, stride=128), :] = rim[i * 16 : i * 16 + 8, half] * (keep[i] * keep_left)
            wide[h, pl.ds(k * 32 + 24, FR, stride=128), :] = rim[i * 16 + 8 : i * 16 + 16, half] * (
                keep[i] * keep_right
            )
        for s in range(3):
            for t in range(2):
                a2[s, t, k] = jnp.zeros((16, C2), BF)
            for t in range(FR):
                base = (t * 4 + k) * 32 + 7 + s
                for h in range(2):
                    a2[s, t + 2, k, :, h * 128 : (h + 1) * 128] = wide[h, base : base + 16].astype(BF)

    blank = jnp.zeros((FR, C2), F32)

    def fix(n, p, s):
        def at(v):
            return jnp.concatenate([beside[h, n, v, 6 + p : 14 + p] for h in range(2)], axis=1)

        rows = ((at(0), at(1), blank, blank), (at(1), blank, blank, at(2)), (blank, blank, at(2), at(3)))[s]
        return jnp.concatenate(rows, axis=0).astype(BF)

    def convolve(q):
        whole = [(i, OUTER.index(i + q)) for i in range(4) if i + q in OUTER]
        left = jnp.concatenate(
            [
                jnp.concatenate(
                    [a2[s, p : p + FR, k].reshape(FR * 16, C2) for _, k in whole] + [fix(n, p, s) for n in range(2)],
                    axis=0,
                )
                for p in range(3)
                for s in range(3)
            ],
            axis=1,
        )
        right = jnp.concatenate([k2[p, q].reshape(3 * C2, C2) for p in range(3)], axis=0)
        got = dot(left, right)
        for h in range(2):
            half = slice(h * 128, (h + 1) * 128)
            for n, (i, _) in enumerate(whole):
                mid[h, i * 128 : (i + 1) * 128] += got[n * 128 : (n + 1) * 128, half]
            for n in range(2):
                for v, j in enumerate(FIXED):
                    at = pl.ds((2 - q + n) * 128 + j, FR, stride=16)
                    mid[h, at, :] += got[256 + n * 32 + v * 8 : 256 + n * 32 + v * 8 + 8, half]

    activate(0)
    activate(1)
    convolve(0)
    activate(2)
    activate(3)
    convolve(2)
    convolve(1)
    for t in range(FR):
        for i in range(4):
            sums = jnp.concatenate(
                [acc[h, t, i + 1] + mid[h, i * 128 + t * 16 : i * 128 + t * 16 + 16] for h in range(2)], axis=1
            )
            out[t, i] = sums.astype(BF)


def in_vmem(shape, dtype):
    return jax.ShapeDtypeStruct(shape, dtype)


def operands(rows):
    return [
        pltpu.VMEM(((FR + 2) * rows * PITCH, C1), F32),
        pltpu.VMEM((FR * rows * CL, C1), F32),
        pltpu.VMEM((FR + 2, rows, 16, C2), BF),
        pltpu.VMEM((FR + 2, rows, 16, C2), BF),
        pltpu.VMEM((3, rows, 16, C2), BF),
        pltpu.VMEM((FR, rows, 16, C2), BF),
    ]


ROWS_SHAPE = in_vmem((FR, HALO, CL, C1), BF)
W_SHAPE = in_vmem((3, 4, 512, C2), BF)
M_SHAPE = in_vmem((512, C2), BF)
ACC_SHAPE = in_vmem((2, FR, 6, 16, 128), F32)
MID_SHAPE = in_vmem((2, 4 * FR * 16, 128), F32)
EDGE_SHAPE = in_vmem((96, C2), F32)
STRIP_SHAPE = in_vmem((6, 16, C2), BF)
PARAMS = pltpu.CompilerParams(vmem_limit_bytes=24 * 2**20)


def in_hbm(x):
    return pltpu.with_memory_space_constraint(x, pltpu.HBM)


def held(*xs):
    return tuple(pltpu.with_memory_space_constraint(x, pltpu.VMEM) for x in xs)


def first_part(feat, k1, proj):
    return pl.pallas_call(
        first_kernel,
        out_shape=(ROWS_SHAPE,) * 3 + (W_SHAPE, M_SHAPE) + tuple(in_vmem(x.shape, x.dtype) for x in (feat, k1)),
        in_specs=[HBM] * 3,
        out_specs=(VM,) * 7,
        scratch_shapes=[
            pltpu.SemaphoreType.DMA((2, FR)),
            pltpu.SemaphoreType.DMA,
            pltpu.VMEM(proj.shape, proj.dtype),
            pltpu.SemaphoreType.DMA((2,)),
        ],
        compiler_params=PARAMS,
        name="first_part",
    )(in_hbm(feat), in_hbm(k1), in_hbm(proj))


def own_part(feat, k1, proj, k2, w, m, feat_in, k1_in):
    return pl.pallas_call(
        own_kernel,
        out_shape=(W_SHAPE, M_SHAPE)
        + tuple(in_vmem(x.shape, x.dtype) for x in (feat, k1))
        + (ACC_SHAPE, EDGE_SHAPE, in_vmem(k2.shape, k2.dtype), MID_SHAPE),
        in_specs=[HBM] * 4 + [VM] * 4,
        out_specs=(VM,) * 8,
        scratch_shapes=[
            pltpu.VMEM(proj.shape, proj.dtype),
            pltpu.SemaphoreType.DMA((2,)),
            pltpu.SemaphoreType.DMA((2,)),
            pltpu.VMEM((2, FR * 2 * 32, 128), F32),
            pltpu.VMEM((3, FR + 2, 2, 16, C2), BF),
        ]
        + operands(RW),
        input_output_aliases={4: 0, 5: 1, 6: 2, 7: 3},
        compiler_params=PARAMS,
        name="own_part",
    )(in_hbm(feat), in_hbm(k1), in_hbm(proj), in_hbm(k2), *held(w, m, feat_in, k1_in))


def near_part(got, w, m, acc, edge):
    return pl.pallas_call(
        near_kernel,
        out_shape=(ACC_SHAPE, EDGE_SHAPE),
        in_specs=[VM] * 5,
        out_specs=(VM,) * 2,
        scratch_shapes=operands(HALO),
        input_output_aliases={3: 0, 4: 1},
        compiler_params=PARAMS,
        name="near_part",
    )(got, w, m, *held(acc, edge))


def far_part(got, got_near, w, m, acc, edge):
    return pl.pallas_call(
        far_kernel,
        out_shape=(ACC_SHAPE, EDGE_SHAPE, STRIP_SHAPE, STRIP_SHAPE),
        in_specs=[VM] * 6,
        out_specs=(VM,) * 4,
        scratch_shapes=operands(HALO) + operands(HALO),
        input_output_aliases={4: 0, 5: 1},
        compiler_params=PARAMS,
        name="far_part",
    )(got, got_near, w, m, *held(acc, edge))


def final_part(last_row, last_col, from_b, pair, acc, edge, k2, mid):
    def kernel(*refs):
        final_kernel(last_row, last_col, *refs)

    return pl.pallas_call(
        kernel,
        out_shape=(in_vmem((FR, 4, 16, C2), BF), ACC_SHAPE, MID_SHAPE),
        in_specs=[VM] * 6,
        out_specs=(VM,) * 3,
        scratch_shapes=[
            pltpu.VMEM((96, C2), F32),
            pltpu.VMEM((2, FR * 4 * 32, 128), F32),
            pltpu.VMEM((3, FR + 2, 4, 16, C2), BF),
            pltpu.VMEM((2, 2, 4, 16, 128), F32),
        ],
        input_output_aliases={2: 1, 5: 2},
        compiler_params=PARAMS,
        name="final_part",
    )(from_b, pair, *held(acc), edge, k2, *held(mid))[0]


def pairs(first, count):
    swaps = []
    for i in range(first, count - 1, 2):
        swaps += [(i, i + 1), (i + 1, i)]
    return swaps


def local(features, kernel_one, projection, kernel_two):
    rows, cols = lax.axis_size("row"), lax.axis_size("col")
    send_b, send_a, send_a_too, w, m, *here = first_part(features, kernel_one, projection)
    far_side = [(i, j) for i, j in pairs(0, rows) if min(i, j) % FAR == 0]
    others = [pair for pair in pairs(0, rows) if pair not in far_side]
    from_a = lax.ppermute(send_a, "row", far_side)
    from_b = lax.ppermute(send_b, "row", pairs(1, rows))
    from_a_too = lax.ppermute(send_a_too, "row", others)
    w, m, _, _, acc, edge, kernel_two, mid = own_part(features, kernel_one, projection, kernel_two, w, m, *here)
    acc, edge = near_part(from_a, w, m, acc, edge)
    acc, edge, to_b, to_a = far_part(from_b, from_a_too, w, m, acc, edge)
    from_b = lax.ppermute(to_b, "col", pairs(1, cols))
    pair = lax.all_gather(to_a, "col", axis_index_groups=[[i, i + 1] for i in range(0, cols, 2)])
    return final_part(rows - 1, cols - 1, from_b, pair, acc, edge, kernel_two, mid)


def solution(mesh):
    return jax.shard_map(
        local,
        mesh=mesh,
        in_specs=(P(None, "row", "col", None), P(), P(), P()),
        out_specs=P(None, "row", "col", None),
        check_vma=False,
    )
```
